32 devices in a mesh: rep: 4 (over y, x), exp: 8 (over z, core).
Axes of the slice: x: 2, y: 2, z: 4, core: 2. Of those that a mesh axis runs over, the one named last changes fastest.
Arguments:
- cotangent: bfloat16 [4096, 4096], P(('rep', 'exp')), may hold values from -0.59765625 to 0.59765625
- routes: int32 [4096, 1], P(('rep', 'exp')), may hold values from 0 to 7; in each aligned block of 128 rows (0 to 127, 128 to 255, ...) at most 24 rows name the same one
- gate_weight: float32 [4096, 1], P(('rep', 'exp')), may hold values from 0.1 to 1
- down_weight: bfloat16 [8, 4096, 768], P('exp'), may hold values from -0.21875 to 0.21875
- saved_pre: bfloat16 [4, 8, 192, 1536], P('rep', 'exp'), may hold values from -6 to 6
Outputs:
- weight_grad: float32 [8, 4096, 768], P('exp', 'rep')
- input_grads: bfloat16 [4, 8, 192, 1536], P('rep', 'exp')
- token_grad: float32 [4096, 1], P(('rep', 'exp'))
The draws below stay inside these ranges and needn't reach their ends.
Inputs may be any that keep to these rules, and one draw needn't show every extreme that they name: `routes`: the rows of one device name each expert at most 24 times; in every draw some device names some expert exactly 24 times.
All inputs are finite; a program needn't handle non-finite values.
Results may differ from the reference program's by a relative error of at most 0.019.
Values may be sent and summed in bfloat16 or wider, within the bound.
No kernel may reach another device: no remote copies, remote signals or barrier semaphores. Data moves between devices by JAX's collectives and lax.ppermute only.
A program may use at most 64 MiB of HBM per device.

```python
import math
import jax
import jax.numpy as jnp
import numpy as np
from jax import lax

D = 4096
FF = 768
TOK_DEV = 128
EXPERTS = 8
CAP = 24
ROWS = 192
TOKENS = 4096
N_REP = 4
N_EXP = 8


def strengthened(values, stream_key, source, target, shards_of, factor):
    def block_of(dim):
        return (jnp.arange(values.shape[dim]) // (values.shape[dim] // shards_of)).reshape((-1,) + (1,) * (values.ndim - 1 - dim))

    one_side = jax.random.permutation(stream_key, shards_of)[block_of(target)]
    second = (block_of(target) + shards_of // 2) % shards_of
    return jnp.where((block_of(source) == one_side) | (block_of(source) == second), factor * values, values)


def block_scale(key, shape, cuts, least, largest):
    gain = 1.0
    for dim, shards_of in cuts:
        draws = jax.random.uniform(jax.random.fold_in(jax.random.fold_in(key, 6), dim), (shards_of,), jnp.float32, least / len(cuts), largest / len(cuts))
        gain = gain * jnp.repeat(jnp.exp(draws), shape[dim] // shards_of).reshape((-1,) + (1,) * (len(shape) - 1 - dim))
    return gain


def routed_block(stream_key, own, number, rows, amount, top, bound, lean):
    ranking = jax.random.permutation(stream_key, amount)
    heavy_load, common = portions_of(amount, rows * top, bound, lean, True), portions_of(amount, rows * top, bound, lean, False)
    places = jnp.arange(amount)

    def named(sizes, rotation):
        used = int((sizes > 0).sum())
        fixed = max(1, used // 4)
        passed = fixed + (places - fixed + rotation * (used - fixed)) % max(1, amount - fixed)
        return jnp.zeros((amount,), jnp.int32).at[ranking[jnp.where(places < fixed, places, passed)]].set(jnp.asarray(sizes, jnp.int32))

    sizes = jnp.where(number % 4 == 0, named(heavy_load, number // 4), named(common, number - number // 4 - 1))
    mixed = jax.random.permutation(jax.random.fold_in(own, 3), amount)
    giver, receiver = mixed[0:amount // 2 * 2:2], mixed[1:amount // 2 * 2:2]
    room = jnp.minimum(sizes[giver] - 1, bound - sizes[receiver]) // 2
    room = jnp.where((giver == ranking[0]) | (receiver == ranking[0]) | (sizes[receiver] == 0), 0, jnp.maximum(room, 0))
    passed = jax.random.randint(jax.random.fold_in(own, 4), (amount // 2,), 0, 1 << 20) % (room + 1)
    sizes = sizes.at[giver].add(-passed).at[receiver].add(passed)
    items = jnp.searchsorted(jnp.cumsum(sizes), jnp.arange(rows * top), side="right").astype(jnp.int32)
    grid = items.reshape(top, rows).T
    grid = grid[jax.random.permutation(jax.random.fold_in(own, 1), rows)]
    rotation = jax.random.randint(jax.random.fold_in(own, 2), (rows, 1), 0, top)
    return jnp.take_along_axis(grid, (jnp.arange(top)[None, :] + rotation) % top, axis=1)


def portions_of(count, total, bound, slope, full):
    portions = [(1 << 20) // math.isqrt(grade ** slope) + 1 for grade in range(1, count + 1)]
    largest = bound if full else min(bound, max(-(-total // count), total * portions[0] // sum(portions)))
    least = 1 if total - largest >= count - 1 else 0
    given, spare = [largest] + [least] * (count - 1), total - largest - least * (count - 1)
    while spare > 0:
        movable = [i for i in range(1, count) if given[i] < largest] or [i for i in range(1, count) if given[i] < bound]
        mass, remaining = sum([portions[i] for i in movable]), spare
        for i in movable:
            addition = min(bound - given[i], max(1, remaining * portions[i] // mass), spare)
            given[i] = given[i] + addition
            spare = spare - addition
    return np.array(given)


def centred(rng, shape, width, limit, cuts=(), held_as=jnp.bfloat16):
    values = jax.random.normal(rng, shape, jnp.float32) * width
    if len(cuts) > 0:
        values = block_scale(rng, shape, cuts, -0.22, 0.18) * values
    return jnp.clip(values, min=-limit, max=limit).astype(held_as)


def bell_draw_with(rng, shape, scale, reach, split, heavy, held_as=jnp.bfloat16):
    entries = scale * jax.random.normal(rng, shape, jnp.float32)
    if split:
        entries = entries * block_scale(rng, shape, split, -0.22, 0.18)
    return jnp.clip(strengthened(entries, jax.random.fold_in(rng, 3), *heavy), -reach, reach).astype(held_as)


def setup_inputs(seed: int = 0) -> dict:
    keys = jax.random.split(jax.random.key(seed), 6)
    cotangent = bell_draw_with(keys[0], (TOKENS, D), 0.1, 0.59765625, ((0, 32),), (0, 1, 32, 2.75))
    routes_keys = jax.random.split(jax.random.fold_in(keys[1], 1), TOKENS // TOK_DEV)
    routes_turns = jax.random.permutation(jax.random.fold_in(keys[1], 3), TOKENS // TOK_DEV)
    routes = jax.vmap(lambda own, number: routed_block(jax.random.fold_in(keys[1], 2), own, number, TOK_DEV, EXPERTS, 1, CAP, 2))(routes_keys, routes_turns).reshape((TOKENS, 1))
    gate_weight = jnp.clip(jnp.exp(math.log(1.0) - 2.3025851 * jax.random.uniform(keys[2], (TOKENS, 1), jnp.float32) ** block_scale(keys[2], (TOKENS, 1), ((0, 32),), -0.2, 0.2)), 0.1, 1.0)
    down_weight = centred(keys[3], (EXPERTS, D, FF), FF ** -0.5, 0.21875, ((0, 8),))
    saved_pre = centred(keys[4], (N_REP, EXPERTS, ROWS, 2 * FF), 1.0, 6.0, ((0, 4), (1, 8)))
    return {"cotangent": cotangent, "routes": routes, "gate_weight": gate_weight, "down_weight": down_weight, "saved_pre": saved_pre}


def slot_table(expert_ids):
    experts = jnp.arange(EXPERTS, dtype=jnp.int32)
    one_hot = (expert_ids[:, :, None] == experts[None, None, :]).astype(jnp.int32)
    earlier = jnp.cumsum(one_hot, axis=1) - one_hot
    position = jnp.sum(earlier * one_hot, axis=2)
    source = jnp.arange(N_EXP, dtype=jnp.int32)[:, None]
    return (source * CAP + position).astype(jnp.int32)


def reference(cotangent, routes, gate_weight, down_weight, saved_pre):
    wide_weight = down_weight.astype(jnp.float32)
    block_rows = N_EXP * TOK_DEV

    def replica(running, replica_index):
        begin_row = replica_index * block_rows
        cot_rows = lax.dynamic_slice_in_dim(cotangent, begin_row, block_rows, 0)
        expert_ids = lax.dynamic_slice_in_dim(routes, begin_row, block_rows, 0)[:, 0].reshape(N_EXP, TOK_DEV)
        weights = lax.dynamic_slice_in_dim(gate_weight, begin_row, block_rows, 0)[:, 0].reshape(N_EXP, TOK_DEV).astype(jnp.bfloat16)
        slot_rows = slot_table(expert_ids)
        arrived = jnp.zeros((EXPERTS, ROWS, D), jnp.bfloat16).at[expert_ids, slot_rows].set(cot_rows.reshape(N_EXP, TOK_DEV, D))
        weight_sent = jnp.zeros((EXPERTS, ROWS), jnp.bfloat16).at[expert_ids, slot_rows].set(weights)
        saved_pair = lax.dynamic_index_in_dim(saved_pre, replica_index, 0, keepdims=False).astype(jnp.float32)
        gate_pre = saved_pair[..., :FF]
        up_pre = saved_pair[..., FF:]
        arrived_wide = arrived.astype(jnp.float32)
        pulled = jnp.einsum('esd,edf->esf', arrived_wide, wide_weight)
        sigmoid_gate = jax.nn.sigmoid(gate_pre)
        silu_gate = gate_pre * sigmoid_gate
        hidden = silu_gate * up_pre
        router = jnp.sum(pulled * hidden, axis=2)
        scale_col = weight_sent.astype(jnp.float32)[..., None]
        hidden_grad = scale_col * pulled
        gate_grad = hidden_grad * up_pre * sigmoid_gate * (1.0 + gate_pre * (1.0 - sigmoid_gate))
        up_grad = hidden_grad * silu_gate
        pair_grads = jnp.concatenate([gate_grad, up_grad], axis=2).astype(jnp.bfloat16)
        scaled = (scale_col * hidden).astype(jnp.bfloat16)
        partial_value = jnp.einsum('esd,esf->edf', arrived_wide, scaled.astype(jnp.float32)).astype(jnp.bfloat16)
        running = running + partial_value.astype(jnp.float32)
        token_part = router[expert_ids, slot_rows].reshape(block_rows, 1)
        return running, (pair_grads, token_part)

    start_sum = jnp.zeros((EXPERTS, D, FF), jnp.float32)
    weight_grad, (input_grads, token_parts) = lax.scan(replica, start_sum, jnp.arange(N_REP, dtype=jnp.int32))
    return weight_grad, input_grads, token_parts.reshape(TOKENS, 1)
```

```python
import jax
import jax.numpy as jnp
from jax import lax
from jax.experimental import pallas as pl
from jax.experimental.pallas import tpu as pltpu
from jax.sharding import PartitionSpec as P

WHOLE_VMEM = pl.BlockSpec(memory_space=pltpu.VMEM)
SMALL = pl.CostEstimate(flops=1024, bytes_accessed=1024, transcendentals=0)
LARGE = pl.CostEstimate(flops=10**10, bytes_accessed=1024, transcendentals=0)


def swap(value, axis, step):
    n = lax.axis_size(axis)
    return lax.ppermute(value, axis, [(i, i ^ step) for i in range(n)])


def kernel_call(kernel, outs, operands, name, cost=SMALL, vmem=24, **more):
    more.setdefault("in_specs", [WHOLE_VMEM] * len(operands))
    more.setdefault("out_specs", [WHOLE_VMEM] * len(outs))
    return pl.pallas_call(
        kernel,
        out_shape=outs,
        compiler_params=pltpu.CompilerParams(vmem_limit_bytes=vmem * 1024 * 1024),
        cost_estimate=cost,
        name=name,
        **more,
    )(*operands)


def prepare_kernel(saved, hidden):
    width = hidden.shape[2]
    for k in range(saved.shape[0]):
        gate = saved[k, :, :width].astype(jnp.float32)
        up = saved[k, :, width:].astype(jnp.float32)
        hidden[k] = (gate / (1.0 + jnp.exp(-gate)) * up).astype(jnp.bfloat16)


def place_kernel(cap, order, cot, cot_sib, routes, routes_sib, weights, weights_sib, *outs):
    chips = len(order)
    blocks, slots_out, last_out = outs[:chips], outs[chips], outs[chips + 1]
    me, mine = lax.axis_index("exp"), lax.axis_index("rep")
    chip, core = me // 2, lax.rem(me, 2)
    replicas, pair, share = blocks[0].shape
    tokens = cot.shape[0]
    before = (
        lax.broadcasted_iota(jnp.int32, (tokens, tokens), 0)
        < lax.broadcasted_iota(jnp.int32, (tokens, tokens), 1)
    ).astype(jnp.bfloat16)
    placements = []
    for i, (ids, gains) in enumerate(((routes, weights), (routes_sib, weights_sib))):
        expert = ids[...]
        weight = gains[...].astype(jnp.bfloat16).astype(jnp.float32)
        hot = lax.broadcasted_iota(jnp.int32, (2 * chips, tokens), 0) == expert
        earlier = jnp.dot(hot.astype(jnp.bfloat16), before, preferred_element_type=jnp.float32)
        position = jnp.sum(jnp.where(hot, earlier, 0.0), axis=0, keepdims=True).astype(jnp.int32)
        source = core if i == 0 else 1 - core
        step = (expert >> 1) ^ chip
        same = (expert & 1) == core
        rank = sum(jnp.where(step == k, i, 0) for i, k in enumerate(order))
        slot = jnp.where(same, rank * pair + source * cap + position, -1)
        slots_out[i : i + 1, :] = slot
        if i == 0:
            last_out[...] = jnp.where(
                step == order[-1], jnp.where(same, position, cap + position), -1
            )
        here = lax.broadcasted_iota(jnp.int32, (chips * pair, tokens), 0) == slot
        placements.append(jnp.where(here, weight, 0.0).astype(jnp.bfloat16))
    placement = jnp.concatenate(placements, axis=1)
    for j in range(replicas):
        columns = pl.ds(pl.multiple_of((mine ^ j) * share, share), share)
        rows = jnp.concatenate([cot[:, columns], cot_sib[:, columns]], axis=0)
        sent = jnp.dot(placement, rows, preferred_element_type=jnp.float32).astype(jnp.bfloat16)
        for k in range(chips):
            blocks[k][j] = sent[k * pair : (k + 1) * pair]


def products(arrived, down):
    mine = lax.axis_index("rep")
    replicas, _, share = arrived[0].shape
    pulled = 0
    for j in range(replicas):
        rows = jnp.concatenate([ref[j] for ref in arrived], axis=0)
        begin = pl.multiple_of((mine ^ j) * share, share)
        pulled += jnp.dot(rows, down[0, pl.ds(begin, share), :], preferred_element_type=jnp.float32)
    return pulled


def gate_parts(saved):
    width = saved.shape[1] // 2
    gate, up = saved[:, :width].astype(jnp.float32), saved[:, width:].astype(jnp.float32)
    sigmoid = 1.0 / (1.0 + jnp.exp(-gate))
    return gate, up, sigmoid


def router_sums(pulled, saved):
    gate, up, sigmoid = gate_parts(saved)
    return lax.dot_general(
        jnp.ones((8, pulled.shape[1]), jnp.float32),
        pulled * (gate * sigmoid * up),
        (((1,), (1,)), ((), ())),
        precision=lax.Precision.HIGHEST,
        preferred_element_type=jnp.float32,
    )[0:1]


def pair_grads(pulled, saved):
    gate, up, sigmoid = gate_parts(saved)
    both = [pulled * up * sigmoid * (1.0 + gate * (1.0 - sigmoid)), pulled * (gate * sigmoid)]
    return jnp.concatenate(both, axis=1).astype(jnp.bfloat16)


def pull_early_kernel(steps, *refs):
    count = len(steps)
    arrived, (down, saved, grads), routers = refs[:count], refs[count : count + 3], refs[count + 3 :]
    chip = lax.axis_index("exp") // 2
    pulled = products(arrived, down)
    pair = arrived[0].shape[1]
    for i, k in enumerate(steps):
        part = pulled[i * pair : (i + 1) * pair]
        routers[i][...] = router_sums(part, saved[chip ^ k])
        grads[chip ^ k] = pair_grads(part, saved[chip ^ k])


def pull_last_kernel(step, arrived, down, saved, pulled, same, other):
    me = lax.axis_index("exp")
    chip, core = me // 2, lax.rem(me, 2)
    pulled[...] = products([arrived], down)
    router = router_sums(pulled[...], saved[chip ^ step])
    cap = router.shape[1] // 2
    same[...] = jnp.where(core == 0, router[:, :cap], router[:, cap:])
    other[...] = jnp.where(core == 0, router[:, cap:], router[:, :cap])


def grads_last_kernel(step, pulled, saved, early, grads):
    chip = lax.axis_index("exp") // 2
    grads[...] = early[...]
    grads[chip ^ step] = pair_grads(pulled[...], saved[chip ^ step])


def stack_kernel(count, *refs):
    for j, out in enumerate(refs[count:]):
        out[...] = jnp.concatenate([ref[j] for ref in refs[:count]], axis=0)


def stack(rows):
    replicas, pair, share = rows[0].shape
    return kernel_call(
        lambda *refs: stack_kernel(len(rows), *refs),
        [jax.ShapeDtypeStruct((len(rows) * pair, share), jnp.bfloat16)] * replicas,
        rows,
        "stack",
    )


def units_of(hidden, steps):
    chip = lax.axis_index("exp") // 2
    return jnp.concatenate([ref[chip ^ k] for ref in hidden for k in steps], axis=0)


def weight_early_kernel(steps, replicas, *refs):
    rows, hidden, out = refs[:replicas], refs[replicas : 2 * replicas], refs[-1]
    out[...] = lax.dot_general(
        jnp.concatenate([ref[...] for ref in rows], axis=0),
        units_of(hidden, steps),
        (((0,), (0,)), ((), ())),
        preferred_element_type=jnp.float32,
    )


def weight_last_kernel(steps, replicas, parts, *refs):
    rows, hidden = refs[:replicas], refs[replicas : 2 * replicas]
    early, out, held, sems = refs[2 * replicas :]
    units = units_of(hidden, steps)
    size = early.shape[0] // parts
    copies = []
    for i in range(parts):
        span = pl.ds(i * size, size)
        left = jnp.concatenate([ref[:, i * size : (i + 1) * size] for ref in rows], axis=0)
        held[span, :] = early[span, :] + lax.dot_general(
            left, units, (((0,), (0,)), ((), ())), preferred_element_type=jnp.float32
        )
        copy = pltpu.make_async_copy(held.at[span, :], out.at[0, span, :], sems.at[i])
        copy.start()
        copies.append(copy)
    for copy in copies:
        copy.wait()


def shards(cotangent, routes, gate_weight, down_weight, saved_pre):
    peers = lax.axis_size("exp")
    replicas = lax.axis_size("rep")
    rows_all = saved_pre.shape[2]
    cap = rows_all // peers
    chips = peers // 2
    pair = 2 * cap
    if pair % 16:
        return plain_shards(cotangent, routes, gate_weight, down_weight, saved_pre)
    width = down_weight.shape[2]
    tokens, model = cotangent.shape
    share = model // replicas

    last = chips // 2
    early = [k for k in range(chips) if k != last]
    order = early + [last]

    routes = routes.reshape(1, tokens)
    weights = gate_weight.reshape(1, tokens)
    cot_sib = swap(cotangent, "exp", 1)
    routes_sib = swap(routes, "exp", 1)
    weights_sib = swap(weights, "exp", 1)
    saved = saved_pre.reshape(chips, pair, 2 * width)
    hidden = kernel_call(
        prepare_kernel,
        [jax.ShapeDtypeStruct((chips, pair, width), jnp.bfloat16)],
        [saved],
        "prepare",
        LARGE,
    )[0]
    hidden, cot_sib = lax.optimization_barrier((hidden, cot_sib))
    *blocks, slots, last_slots = kernel_call(
        lambda *refs: place_kernel(cap, order, *refs),
        [jax.ShapeDtypeStruct((replicas, pair, share), jnp.bfloat16)] * chips
        + [
            jax.ShapeDtypeStruct((2, tokens), jnp.int32),
            jax.ShapeDtypeStruct((1, tokens), jnp.int32),
        ],
        [cotangent, cot_sib, routes, routes_sib, weights, weights_sib],
        "place",
    )

    blocks = dict(zip(order, blocks))
    arrived = {0: blocks[0]}
    for k in reversed(early[1:]):
        arrived[k] = swap(blocks[k], "exp", 2 * k)
    hidden_of = [hidden] + [swap(hidden, "rep", j) for j in range(1, replicas)]

    rows, last_block, hidden_of = lax.optimization_barrier(
        ([arrived[k] for k in early], blocks[last], hidden_of)
    )
    arrived = dict(zip(early, rows))
    arrived[last] = swap(last_block, "exp", 2 * last)
    early_rows = stack(rows)
    early_rows = [early_rows[0]] + [swap(early_rows[j], "rep", j) for j in range(1, replicas)]
    grads, *routers = kernel_call(
        lambda *refs: pull_early_kernel(early, *refs),
        [jax.ShapeDtypeStruct(saved.shape, jnp.bfloat16)]
        + [jax.ShapeDtypeStruct((1, pair), jnp.float32)] * len(early),
        [*[arrived[k] for k in early], down_weight, saved],
        "pull_early",
    )
    returned = routers[:1] + [swap(router, "exp", 2 * k) for router, k in zip(routers[1:], early[1:])]
    total = kernel_call(
        lambda *refs: weight_early_kernel(early, replicas, *refs),
        [jax.ShapeDtypeStruct((share, width), jnp.float32)],
        [*early_rows, *hidden_of],
        "weight_early",
    )[0]

    arrived[last], grads, total, returned = lax.optimization_barrier(
        (arrived[last], grads, total, returned)
    )
    rows = arrived[last]
    late_rows = [rows[0]] + [swap(rows[j], "rep", j) for j in range(1, replicas)]
    pulled, *routers = kernel_call(
        lambda *refs: pull_last_kernel(last, *refs),
        [jax.ShapeDtypeStruct((pair, width), jnp.float32)]
        + [jax.ShapeDtypeStruct((1, cap), jnp.float32)] * 2,
        [arrived[last], down_weight, saved],
        "pull_last",
    )
    returned = jnp.concatenate(returned, axis=1).reshape(len(early) * pair, 1)
    slot_index = lax.broadcasted_iota(jnp.int32, (len(early) * pair, 1), 0)
    sums = [
        jnp.sum(jnp.where(slot_index == slots[i][None, :], returned, 0.0), axis=0)
        for i in range(2)
    ]
    sum_sib = swap(sums[1], "exp", 1)
    routers, sum_sib = lax.optimization_barrier((routers, sum_sib))
    returned_last = [swap(routers[i], "exp", 2 * last + i) for i in range(2)]
    weight_grad = kernel_call(
        lambda *refs: weight_last_kernel([last], replicas, 4, *refs),
        jax.ShapeDtypeStruct((1, share, width), jnp.float32),
        [*late_rows, *hidden_of, total],
        "weight_last",
        LARGE,
        out_specs=pl.BlockSpec(memory_space=pl.ANY),
        scratch_shapes=[pltpu.VMEM((share, width), jnp.float32), pltpu.SemaphoreType.DMA((4,))],
    )
    weight_grad, pulled = lax.optimization_barrier((weight_grad, pulled))
    grads = kernel_call(
        lambda *refs: grads_last_kernel(last, *refs),
        [jax.ShapeDtypeStruct(saved.shape, jnp.bfloat16)],
        [pulled, saved, grads],
        "grads_last",
    )[0]
    returned_last, grads = lax.optimization_barrier((returned_last, grads))
    returned = jnp.concatenate(returned_last, axis=1).reshape(pair, 1)
    slot_index = lax.broadcasted_iota(jnp.int32, (pair, 1), 0)
    last_sum = jnp.sum(jnp.where(slot_index == last_slots, returned, 0.0), axis=0)
    token_grad = (sums[0] + sum_sib + last_sum) / weights[0].astype(jnp.bfloat16).astype(jnp.float32)
    return (weight_grad, grads.reshape(1, 1, rows_all, 2 * width), token_grad[:, None])


def plain_shards(cotangent, routes, gate_weight, down_weight, saved_pre):
    peers = lax.axis_size("exp")
    replicas = lax.axis_size("rep")
    me = lax.axis_index("exp")
    mine = lax.axis_index("rep")
    rows_all = saved_pre.shape[2]
    capacity = rows_all // peers
    width = down_weight.shape[2]
    model = cotangent.shape[1]
    share = model // replicas

    expert_ids = routes[:, 0]
    experts = lax.broadcasted_iota(jnp.int32, (1, peers), 1)
    one_hot = (expert_ids[:, None] == experts).astype(jnp.int32)
    earlier = jnp.cumsum(one_hot, axis=0) - one_hot
    position = jnp.sum(earlier * one_hot, axis=1)
    slot_ids = (expert_ids ^ me) * capacity + position
    slot_index = lax.broadcasted_iota(jnp.int32, (rows_all, 1), 0)
    placement = slot_index == slot_ids[None, :]
    weight = gate_weight[:, 0].astype(jnp.bfloat16)
    outgoing = jnp.dot(
        jnp.where(placement, weight[None, :], 0), cotangent, preferred_element_type=jnp.float32
    ).astype(jnp.bfloat16)
    outgoing = outgoing.reshape(peers, capacity, model)

    groups = [
        list(range(0, peers // 2)),
        list(range(peers // 2, peers // 4 * 3)),
        list(range(peers // 4 * 3, peers)),
    ]
    arrived = {0: outgoing[0]}
    for k in groups[1] + groups[2] + groups[0][1:]:
        arrived[k] = swap(outgoing[k], "exp", k)

    saved = saved_pre[0, 0].reshape(peers, capacity, 2 * width)
    saved = jnp.take(saved, jnp.arange(peers) ^ me, axis=0).reshape(rows_all, 2 * width)
    saved = saved.astype(jnp.float32)
    gate_pre = saved[:, :width]
    up_pre = saved[:, width:]
    sigmoid_gate = jax.nn.sigmoid(gate_pre)
    silu_gate = gate_pre * sigmoid_gate
    hidden = silu_gate * up_pre
    hidden_sent = hidden.astype(jnp.bfloat16)
    hidden_of = [hidden_sent] + [swap(hidden_sent, "rep", j) for j in range(1, replicas)]
    gate_factor = up_pre * sigmoid_gate * (1.0 + gate_pre * (1.0 - sigmoid_gate))

    total = 0
    pulled_parts = []
    returned = []
    for group in groups:
        begin, end = group[0] * capacity, (group[-1] + 1) * capacity
        rows = jnp.concatenate([arrived[k] for k in group], axis=0)
        columns = [
            lax.dynamic_slice_in_dim(rows, (mine ^ j) * share, share, 1) for j in range(replicas)
        ]
        left = [columns[0]] + [swap(columns[j], "rep", j) for j in range(1, replicas)]
        right = [hidden_of[j][begin:end] for j in range(replicas)]
        total = total + lax.dot_general(
            jnp.concatenate(left, axis=0),
            jnp.concatenate(right, axis=0),
            (((0,), (0,)), ((), ())),
            preferred_element_type=jnp.float32,
        )
        pulled = jnp.dot(rows, down_weight[0], preferred_element_type=jnp.float32)
        pulled_parts.append(pulled)
        router = jnp.sum(pulled * hidden[begin:end], axis=1).reshape(len(group), capacity)
        returned += [router[i] if k == 0 else swap(router[i], "exp", k) for i, k in enumerate(group)]
    pulled = jnp.concatenate(pulled_parts, axis=0)
    pair_grads = jnp.concatenate([pulled * gate_factor, pulled * silu_gate], axis=1).astype(
        jnp.bfloat16
    )
    pair_grads = pair_grads.reshape(peers, capacity, 2 * width)
    pair_grads = jnp.take(pair_grads, jnp.arange(peers) ^ me, axis=0)
    returned_grad = jnp.concatenate(returned, axis=0)
    token_grad = jnp.sum(jnp.where(placement, returned_grad[:, None], 0.0), axis=0)
    token_grad = token_grad / weight.astype(jnp.float32)
    return (
        total[None],
        pair_grads.reshape(1, 1, rows_all, 2 * width),
        token_grad[:, None],
    )


def solution(mesh):
    in_specs = (
        P(("rep", "exp"), None),
        P(("rep", "exp"), None),
        P(("rep", "exp"), None),
        P("exp", None, None),
        P("rep", "exp", None, None),
    )
    out_specs = (P("exp", "rep", None), P("rep", "exp", None, None), P(("rep", "exp"), None))
    return jax.shard_map(shards, mesh=mesh, in_specs=in_specs, out_specs=out_specs, check_vma=False)
```

```python
import jax
import jax.numpy as jnp
from jax import lax
from jax.experimental import pallas as pl
from jax.experimental.pallas import tpu as pltpu
from jax.sharding import PartitionSpec as P

WHOLE_VMEM = pl.BlockSpec(memory_space=pltpu.VMEM)
IN_PLACE = pl.BlockSpec(memory_space=pl.ANY)
SMALL = pl.CostEstimate(flops=1024, bytes_accessed=1024, transcendentals=0)
LARGE = pl.CostEstimate(flops=10**10, bytes_accessed=1024, transcendentals=0)


def swap(value, axis, step):
    n = lax.axis_size(axis)
    return lax.ppermute(value, axis, [(i, i ^ step) for i in range(n)])


def kernel_call(kernel, outs, operands, name, cost=SMALL, vmem=24, **more):
    more.setdefault("in_specs", [WHOLE_VMEM] * len(operands))
    more.setdefault("out_specs", [WHOLE_VMEM] * len(outs))
    return pl.pallas_call(
        kernel,
        out_shape=outs,
        compiler_params=pltpu.CompilerParams(vmem_limit_bytes=vmem * 1024 * 1024),
        cost_estimate=cost,
        name=name,
        **more,
    )(*operands)


def copy_kernel(rows, out):
    out[...] = rows[...]


def hidden_kernel(saved, hidden):
    for k in range(saved.shape[0]):
        gate, up, sigmoid = gate_parts(saved[k])
        hidden[k] = (gate * sigmoid * up).astype(jnp.bfloat16)


def place_kernel(cap, order, cot, cot_sib, routes, routes_sib, weights, weights_sib, *outs):
    chips = len(order)
    blocks, slots_out, last_out = outs[:chips], outs[chips], outs[chips + 1]
    me, mine = lax.axis_index("exp"), lax.axis_index("rep")
    chip, core = me // 2, lax.rem(me, 2)
    replicas, pair, share = blocks[0].shape
    tokens = cot.shape[0]
    before = (
        lax.broadcasted_iota(jnp.int32, (tokens, tokens), 0)
        < lax.broadcasted_iota(jnp.int32, (tokens, tokens), 1)
    ).astype(jnp.bfloat16)
    placements = []
    for i, (ids, gains) in enumerate(((routes, weights), (routes_sib, weights_sib))):
        expert = ids[...]
        weight = gains[...].astype(jnp.bfloat16).astype(jnp.float32)
        hot = lax.broadcasted_iota(jnp.int32, (2 * chips, tokens), 0) == expert
        earlier = jnp.dot(hot.astype(jnp.bfloat16), before, preferred_element_type=jnp.float32)
        position = jnp.sum(jnp.where(hot, earlier, 0.0), axis=0, keepdims=True).astype(jnp.int32)
        source = core if i == 0 else 1 - core
        step = (expert >> 1) ^ chip
        same = (expert & 1) == core
        rank = sum(jnp.where(step == k, i, 0) for i, k in enumerate(order))
        slot = jnp.where(same, rank * pair + source * cap + position, -1)
        slots_out[i : i + 1, :] = slot
        if i == 0:
            last_out[...] = jnp.where(
                step == order[-1], jnp.where(same, position, cap + position), -1
            )
        here = lax.broadcasted_iota(jnp.int32, (chips * pair, tokens), 0) == slot
        placements.append(jnp.where(here, weight, 0.0).astype(jnp.bfloat16))
    placement = jnp.concatenate(placements, axis=1)
    for j in range(replicas):
        columns = pl.ds(pl.multiple_of((mine ^ j) * share, share), share)
        rows = jnp.concatenate([cot[:, columns], cot_sib[:, columns]], axis=0)
        sent = jnp.dot(placement, rows, preferred_element_type=jnp.float32).astype(jnp.bfloat16)
        for k in range(chips):
            blocks[k][j] = sent[k * pair : (k + 1) * pair]


def products(arrived, down):
    mine = lax.axis_index("rep")
    replicas, _, share = arrived[0].shape
    pulled = 0
    for j in range(replicas):
        rows = jnp.concatenate([ref[j] for ref in arrived], axis=0)
        begin = pl.multiple_of((mine ^ j) * share, share)
        pulled += jnp.dot(rows, down[0, pl.ds(begin, share), :], preferred_element_type=jnp.float32)
    return pulled


def gate_parts(saved):
    width = saved.shape[1] // 2
    gate, up = saved[:, :width].astype(jnp.float32), saved[:, width:].astype(jnp.float32)
    sigmoid = 1.0 / (1.0 + jnp.exp(-gate))
    return gate, up, sigmoid


def router_sums(pulled, saved):
    gate, up, sigmoid = gate_parts(saved)
    return lax.dot_general(
        jnp.ones((8, pulled.shape[1]), jnp.float32),
        pulled * (gate * sigmoid * up),
        (((1,), (1,)), ((), ())),
        precision=lax.Precision.HIGHEST,
        preferred_element_type=jnp.float32,
    )[0:1]


def pair_grads(pulled, saved):
    gate, up, sigmoid = gate_parts(saved)
    both = [pulled * up * sigmoid * (1.0 + gate * (1.0 - sigmoid)), pulled * (gate * sigmoid)]
    return jnp.concatenate(both, axis=1).astype(jnp.bfloat16)


def pull_early_kernel(steps, *refs):
    count = len(steps)
    arrived, (down, saved, grads), routers = refs[:count], refs[count : count + 3], refs[count + 3 :]
    chip = lax.axis_index("exp") // 2
    pulled = products(arrived, down)
    pair = arrived[0].shape[1]
    for i, k in enumerate(steps):
        part = pulled[i * pair : (i + 1) * pair]
        routers[i][...] = router_sums(part, saved[chip ^ k])
        grads[chip ^ k] = pair_grads(part, saved[chip ^ k])


def pull_last_kernel(step, arrived, down, saved, pulled, same, other):
    me = lax.axis_index("exp")
    chip, core = me // 2, lax.rem(me, 2)
    pulled[...] = products([arrived], down)
    router = router_sums(pulled[...], saved[chip ^ step])
    cap = router.shape[1] // 2
    same[...] = jnp.where(core == 0, router[:, :cap], router[:, cap:])
    other[...] = jnp.where(core == 0, router[:, cap:], router[:, :cap])


def stack_kernel(count, *refs):
    for j, out in enumerate(refs[count:]):
        out[...] = jnp.concatenate([ref[j] for ref in refs[:count]], axis=0)


def stack(rows):
    replicas, pair, share = rows[0].shape
    return kernel_call(
        lambda *refs: stack_kernel(len(rows), *refs),
        [jax.ShapeDtypeStruct((len(rows) * pair, share), jnp.bfloat16)] * replicas,
        rows,
        "stack",
    )


def units_kernel(order, *refs):
    hidden, early, late = refs[:-2], refs[-2], refs[-1]
    chip = lax.axis_index("exp") // 2
    early[...] = jnp.concatenate([ref[chip ^ k] for ref in hidden for k in order[:-1]], axis=0)
    late[...] = jnp.concatenate([ref[chip ^ order[-1]] for ref in hidden], axis=0)


def weight_early_kernel(*refs):
    rows, units, out = refs[:-2], refs[-2], refs[-1]
    out[...] = lax.dot_general(
        jnp.concatenate([ref[...] for ref in rows], axis=0),
        units[...],
        (((0,), (0,)), ((), ())),
        preferred_element_type=jnp.float32,
    )


def finish_kernel(step, replicas, parts, *refs):
    rows = refs[:replicas]
    units, early, pulled, saved, _, out, grads, held, held_grads, sems = refs[replicas:]
    size = early.shape[0] // parts
    copies = []
    for i in range(parts):
        span = pl.ds(i * size, size)
        left = jnp.concatenate([ref[:, i * size : (i + 1) * size] for ref in rows], axis=0)
        held[span, :] = early[span, :] + lax.dot_general(
            left, units[...], (((0,), (0,)), ((), ())), preferred_element_type=jnp.float32
        )
        copies.append(pltpu.make_async_copy(held.at[span, :], out.at[0, span, :], sems.at[i]))
        copies[-1].start()
        if i == 0:
            place = (lax.axis_index("exp") // 2) ^ step
            held_grads[...] = pair_grads(pulled[...], saved[place])
            copies.append(pltpu.make_async_copy(held_grads, grads.at[place], sems.at[parts]))
            copies[-1].start()
    for copy in copies:
        copy.wait()


def token_kernel(same, other, last_slots, own, sib, weights, out):
    values = jnp.concatenate([same[...], other[...]], axis=1)
    hot = lax.broadcasted_iota(jnp.int32, (values.shape[1], out.shape[1]), 0) == last_slots[...]
    found = lax.dot_general(
        jnp.broadcast_to(values, (8, values.shape[1])),
        hot.astype(jnp.float32),
        (((1,), (0,)), ((), ())),
        precision=lax.Precision.HIGHEST,
        preferred_element_type=jnp.float32,
    )[0:1]
    weight = weights[...].astype(jnp.bfloat16).astype(jnp.float32)
    out[...] = (own[...] + sib[...] + found) / weight


def shards(cotangent, routes, gate_weight, down_weight, saved_pre):
    peers = lax.axis_size("exp")
    replicas = lax.axis_size("rep")
    rows_all = saved_pre.shape[2]
    cap = rows_all // peers
    chips = peers // 2
    pair = 2 * cap
    if pair % 16:
        return plain_shards(cotangent, routes, gate_weight, down_weight, saved_pre)
    width = down_weight.shape[2]
    tokens, model = cotangent.shape
    share = model // replicas

    last = chips // 2
    early = [k for k in range(chips) if k != last]
    order = early + [last]

    routes = routes.reshape(1, tokens)
    weights = gate_weight.reshape(1, tokens)
    cot_sib = swap(cotangent, "exp", 1)
    routes_sib = swap(routes, "exp", 1)
    weights_sib = swap(weights, "exp", 1)
    own_rows = kernel_call(
        copy_kernel,
        [jax.ShapeDtypeStruct((tokens, model), jnp.bfloat16)],
        [cotangent],
        "own_rows",
        LARGE,
    )[0]
    *blocks, slots, last_slots = kernel_call(
        lambda *refs: place_kernel(cap, order, *refs),
        [jax.ShapeDtypeStruct((replicas, pair, share), jnp.bfloat16)] * chips
        + [
            jax.ShapeDtypeStruct((2, tokens), jnp.int32),
            jax.ShapeDtypeStruct((1, tokens), jnp.int32),
        ],
        [own_rows, cot_sib, routes, routes_sib, weights, weights_sib],
        "place",
    )

    blocks = dict(zip(order, blocks))
    arrived = {0: blocks[0]}
    for k in reversed(early[1:]):
        arrived[k] = swap(blocks[k], "exp", 2 * k)
    saved = saved_pre.reshape(chips, pair, 2 * width)
    saved, slots = lax.optimization_barrier((saved, slots))
    hidden = kernel_call(
        hidden_kernel,
        [jax.ShapeDtypeStruct((chips, pair, width), jnp.bfloat16)],
        [saved],
        "hidden",
    )[0]
    hidden_of = [hidden] + [swap(hidden, "rep", j) for j in range(1, replicas)]
    units, units_last = kernel_call(
        lambda *refs: units_kernel(order, *refs),
        [
            jax.ShapeDtypeStruct((replicas * len(early) * pair, width), jnp.bfloat16),
            jax.ShapeDtypeStruct((replicas * pair, width), jnp.bfloat16),
        ],
        hidden_of,
        "units",
    )

    rows, last_block, units = lax.optimization_barrier(
        ([arrived[k] for k in early], blocks[last], units)
    )
    arrived = dict(zip(early, rows))
    last_rows = swap(last_block, "exp", 2 * last)
    early_rows = stack(rows)
    early_rows = [early_rows[0]] + [swap(early_rows[j], "rep", j) for j in range(1, replicas)]
    grads, *routers = kernel_call(
        lambda *refs: pull_early_kernel(early, *refs),
        [jax.ShapeDtypeStruct(saved.shape, jnp.bfloat16)]
        + [jax.ShapeDtypeStruct((1, pair), jnp.float32)] * len(early),
        [*[arrived[k] for k in early], down_weight, saved],
        "pull_early",
    )
    returned = routers[:1] + [swap(router, "exp", 2 * k) for router, k in zip(routers[1:], early[1:])]
    total = kernel_call(
        weight_early_kernel,
        [jax.ShapeDtypeStruct((share, width), jnp.float32)],
        [*early_rows, units],
        "weight_early",
    )[0]

    rows, grads, total, returned = lax.optimization_barrier((last_rows, grads, total, returned))
    late_rows = [rows[0]] + [swap(rows[j], "rep", j) for j in range(1, replicas)]
    pulled, *routers = kernel_call(
        lambda *refs: pull_last_kernel(last, *refs),
        [jax.ShapeDtypeStruct((pair, width), jnp.float32)]
        + [jax.ShapeDtypeStruct((1, cap), jnp.float32)] * 2,
        [rows, down_weight, saved],
        "pull_last",
    )
    returned = jnp.concatenate(returned, axis=1).reshape(len(early) * pair, 1)
    slot_index = lax.broadcasted_iota(jnp.int32, (len(early) * pair, 1), 0)
    sums = [
        jnp.sum(jnp.where(slot_index == ids, returned, 0.0), axis=0, keepdims=True)
        for ids in (slots[0:1], slots[1:2])
    ]
    sum_sib = swap(sums[1], "exp", 1)
    routers, sum_sib = lax.optimization_barrier((routers, sum_sib))
    returned_last = [swap(routers[i], "exp", 2 * last + i) for i in range(2)]
    parts = 4
    weight_grad, grads = kernel_call(
        lambda *refs: finish_kernel(last, replicas, parts, *refs),
        [
            jax.ShapeDtypeStruct((1, share, width), jnp.float32),
            jax.ShapeDtypeStruct(saved.shape, jnp.bfloat16),
        ],
        [*late_rows, units_last, total, pulled, saved, grads],
        "finish",
        LARGE,
        in_specs=[WHOLE_VMEM] * (replicas + 4) + [IN_PLACE],
        out_specs=[IN_PLACE] * 2,
        input_output_aliases={replicas + 4: 1},
        scratch_shapes=[
            pltpu.VMEM((share, width), jnp.float32),
            pltpu.VMEM((pair, 2 * width), jnp.bfloat16),
            pltpu.SemaphoreType.DMA((parts + 1,)),
        ],
    )
    returned_last, weight_grad = lax.optimization_barrier((returned_last, weight_grad))
    token_grad = kernel_call(
        token_kernel,
        [jax.ShapeDtypeStruct((1, tokens), jnp.float32)],
        [*returned_last, last_slots, sums[0], sum_sib, weights],
        "token",
    )[0]
    return (weight_grad, grads.reshape(1, 1, rows_all, 2 * width), token_grad.reshape(tokens, 1))


def plain_shards(cotangent, routes, gate_weight, down_weight, saved_pre):
    peers = lax.axis_size("exp")
    replicas = lax.axis_size("rep")
    me = lax.axis_index("exp")
    mine = lax.axis_index("rep")
    rows_all = saved_pre.shape[2]
    capacity = rows_all // peers
    width = down_weight.shape[2]
    model = cotangent.shape[1]
    share = model // replicas

    expert_ids = routes[:, 0]
    experts = lax.broadcasted_iota(jnp.int32, (1, peers), 1)
    one_hot = (expert_ids[:, None] == experts).astype(jnp.int32)
    earlier = jnp.cumsum(one_hot, axis=0) - one_hot
    position = jnp.sum(earlier * one_hot, axis=1)
    slot_ids = (expert_ids ^ me) * capacity + position
    slot_index = lax.broadcasted_iota(jnp.int32, (rows_all, 1), 0)
    placement = slot_index == slot_ids[None, :]
    weight = gate_weight[:, 0].astype(jnp.bfloat16)
    outgoing = jnp.dot(
        jnp.where(placement, weight[None, :], 0), cotangent, preferred_element_type=jnp.float32
    ).astype(jnp.bfloat16)
    outgoing = outgoing.reshape(peers, capacity, model)

    groups = [
        list(range(0, peers // 2)),
        list(range(peers // 2, peers // 4 * 3)),
        list(range(peers // 4 * 3, peers)),
    ]
    arrived = {0: outgoing[0]}
    for k in groups[1] + groups[2] + groups[0][1:]:
        arrived[k] = swap(outgoing[k], "exp", k)

    saved = saved_pre[0, 0].reshape(peers, capacity, 2 * width)
    saved = jnp.take(saved, jnp.arange(peers) ^ me, axis=0).reshape(rows_all, 2 * width)
    saved = saved.astype(jnp.float32)
    gate_pre = saved[:, :width]
    up_pre = saved[:, width:]
    sigmoid_gate = jax.nn.sigmoid(gate_pre)
    silu_gate = gate_pre * sigmoid_gate
    hidden = silu_gate * up_pre
    hidden_sent = hidden.astype(jnp.bfloat16)
    hidden_of = [hidden_sent] + [swap(hidden_sent, "rep", j) for j in range(1, replicas)]
    gate_factor = up_pre * sigmoid_gate * (1.0 + gate_pre * (1.0 - sigmoid_gate))

    total = 0
    pulled_parts = []
    returned = []
    for group in groups:
        begin, end = group[0] * capacity, (group[-1] + 1) * capacity
        rows = jnp.concatenate([arrived[k] for k in group], axis=0)
        columns = [
            lax.dynamic_slice_in_dim(rows, (mine ^ j) * share, share, 1) for j in range(replicas)
        ]
        left = [columns[0]] + [swap(columns[j], "rep", j) for j in range(1, replicas)]
        right = [hidden_of[j][begin:end] for j in range(replicas)]
        total = total + lax.dot_general(
            jnp.concatenate(left, axis=0),
            jnp.concatenate(right, axis=0),
            (((0,), (0,)), ((), ())),
            preferred_element_type=jnp.float32,
        )
        pulled = jnp.dot(rows, down_weight[0], preferred_element_type=jnp.float32)
        pulled_parts.append(pulled)
        router = jnp.sum(pulled * hidden[begin:end], axis=1).reshape(len(group), capacity)
        returned += [router[i] if k == 0 else swap(router[i], "exp", k) for i, k in enumerate(group)]
    pulled = jnp.concatenate(pulled_parts, axis=0)
    pair_grads = jnp.concatenate([pulled * gate_factor, pulled * silu_gate], axis=1).astype(
        jnp.bfloat16
    )
    pair_grads = pair_grads.reshape(peers, capacity, 2 * width)
    pair_grads = jnp.take(pair_grads, jnp.arange(peers) ^ me, axis=0)
    returned_grad = jnp.concatenate(returned, axis=0)
    token_grad = jnp.sum(jnp.where(placement, returned_grad[:, None], 0.0), axis=0)
    token_grad = token_grad / weight.astype(jnp.float32)
    return (
        total[None],
        pair_grads.reshape(1, 1, rows_all, 2 * width),
        token_grad[:, None],
    )


def solution(mesh):
    in_specs = (
        P(("rep", "exp"), None),
        P(("rep", "exp"), None),
        P(("rep", "exp"), None),
        P("exp", None, None),
        P("rep", "exp", None, None),
    )
    out_specs = (P("exp", "rep", None), P("rep", "exp", None, None), P(("rep", "exp"), None))
    return jax.shard_map(shards, mesh=mesh, in_specs=in_specs, out_specs=out_specs, check_vma=False)
```

```python
import jax
import jax.numpy as jnp
from jax import lax
from jax.experimental import pallas as pl
from jax.experimental.pallas import tpu as pltpu
from jax.sharding import PartitionSpec as P

WHOLE_VMEM = pl.BlockSpec(memory_space=pltpu.VMEM)
IN_PLACE = pl.BlockSpec(memory_space=pl.ANY)
SMALL = pl.CostEstimate(flops=1024, bytes_accessed=1024, transcendentals=0)
LARGE = pl.CostEstimate(flops=10**10, bytes_accessed=1024, transcendentals=0)


def swap(value, axis, step):
    n = lax.axis_size(axis)
    return lax.ppermute(value, axis, [(i, i ^ step) for i in range(n)])


def kernel_call(kernel, outs, operands, name, cost=SMALL, vmem=24, **more):
    more.setdefault("in_specs", [WHOLE_VMEM] * len(operands))
    more.setdefault("out_specs", [WHOLE_VMEM] * len(outs))
    return pl.pallas_call(
        kernel,
        out_shape=outs,
        compiler_params=pltpu.CompilerParams(vmem_limit_bytes=vmem * 1024 * 1024),
        cost_estimate=cost,
        name=name,
        **more,
    )(*operands)


def copy_kernel(rows, out):
    out[...] = rows[...]


def hidden_kernel(saved, hidden):
    for k in range(saved.shape[0]):
        gate, up, sigmoid = gate_parts(saved[k])
        hidden[k] = (gate * sigmoid * up).astype(jnp.bfloat16)


def place_kernel(cap, order, cot, cot_sib, routes, routes_sib, weights, weights_sib, *outs):
    chips = len(order)
    blocks, slots_out, last_out = outs[:chips], outs[chips], outs[chips + 1]
    me, mine = lax.axis_index("exp"), lax.axis_index("rep")
    chip, core = me // 2, lax.rem(me, 2)
    replicas, pair, share = blocks[0].shape
    tokens = cot.shape[0]
    before = (
        lax.broadcasted_iota(jnp.int32, (tokens, tokens), 0)
        < lax.broadcasted_iota(jnp.int32, (tokens, tokens), 1)
    ).astype(jnp.bfloat16)
    placements = []
    for i, (ids, gains) in enumerate(((routes, weights), (routes_sib, weights_sib))):
        expert = ids[...]
        weight = gains[...].astype(jnp.bfloat16).astype(jnp.float32)
        hot = lax.broadcasted_iota(jnp.int32, (2 * chips, tokens), 0) == expert
        earlier = jnp.dot(hot.astype(jnp.bfloat16), before, preferred_element_type=jnp.float32)
        position = jnp.sum(jnp.where(hot, earlier, 0.0), axis=0, keepdims=True).astype(jnp.int32)
        source = core if i == 0 else 1 - core
        step = (expert >> 1) ^ chip
        same = (expert & 1) == core
        rank = sum(jnp.where(step == k, i, 0) for i, k in enumerate(order))
        slot = jnp.where(same, rank * pair + source * cap + position, -1)
        slots_out[i : i + 1, :] = slot
        if i == 0:
            last_out[...] = jnp.where(
                step == order[-1], jnp.where(same, position, cap + position), -1
            )
        here = lax.broadcasted_iota(jnp.int32, (chips * pair, tokens), 0) == slot
        placements.append(jnp.where(here, weight, 0.0).astype(jnp.bfloat16))
    placement = jnp.concatenate(placements, axis=1)
    for j in range(replicas):
        columns = pl.ds(pl.multiple_of((mine ^ j) * share, share), share)
        rows = jnp.concatenate([cot[:, columns], cot_sib[:, columns]], axis=0)
        sent = jnp.dot(placement, rows, preferred_element_type=jnp.float32).astype(jnp.bfloat16)
        for k in range(chips):
            blocks[k][j] = sent[k * pair : (k + 1) * pair]


def products(arrived, down):
    mine = lax.axis_index("rep")
    replicas, _, share = arrived[0].shape
    pulled = 0
    for j in range(replicas):
        rows = jnp.concatenate([ref[j] for ref in arrived], axis=0)
        begin = pl.multiple_of((mine ^ j) * share, share)
        pulled += jnp.dot(rows, down[0, pl.ds(begin, share), :], preferred_element_type=jnp.float32)
    return pulled


def gate_parts(saved):
    width = saved.shape[1] // 2
    gate, up = saved[:, :width].astype(jnp.float32), saved[:, width:].astype(jnp.float32)
    sigmoid = 1.0 / (1.0 + jnp.exp(-gate))
    return gate, up, sigmoid


def router_sums(pulled, saved):
    gate, up, sigmoid = gate_parts(saved)
    return lax.dot_general(
        jnp.ones((8, pulled.shape[1]), jnp.float32),
        pulled * (gate * sigmoid * up),
        (((1,), (1,)), ((), ())),
        precision=lax.Precision.HIGHEST,
        preferred_element_type=jnp.float32,
    )[0:1]


def pair_grads(pulled, saved):
    gate, up, sigmoid = gate_parts(saved)
    both = [pulled * up * sigmoid * (1.0 + gate * (1.0 - sigmoid)), pulled * (gate * sigmoid)]
    return jnp.concatenate(both, axis=1).astype(jnp.bfloat16)


def pull_early_kernel(steps, *refs):
    count = len(steps)
    arrived, (down, saved, grads), routers = refs[:count], refs[count : count + 3], refs[count + 3 :]
    chip = lax.axis_index("exp") // 2
    pulled = products(arrived, down)
    pair = arrived[0].shape[1]
    for i, k in enumerate(steps):
        part = pulled[i * pair : (i + 1) * pair]
        routers[i][...] = router_sums(part, saved[chip ^ k])
        grads[chip ^ k] = pair_grads(part, saved[chip ^ k])


def pull_last_kernel(step, arrived, down, saved, pulled, same, other):
    me = lax.axis_index("exp")
    chip, core = me // 2, lax.rem(me, 2)
    pulled[...] = products([arrived], down)
    router = router_sums(pulled[...], saved[chip ^ step])
    cap = router.shape[1] // 2
    same[...] = jnp.where(core == 0, router[:, :cap], router[:, cap:])
    other[...] = jnp.where(core == 0, router[:, cap:], router[:, :cap])


def stack_kernel(count, *refs):
    for j, out in enumerate(refs[count:]):
        out[...] = jnp.concatenate([ref[j] for ref in refs[:count]], axis=0)


def stack(rows):
    replicas, pair, share = rows[0].shape
    return kernel_call(
        lambda *refs: stack_kernel(len(rows), *refs),
        [jax.ShapeDtypeStruct((len(rows) * pair, share), jnp.bfloat16)] * replicas,
        rows,
        "stack",
    )


def units_kernel(order, *refs):
    hidden, early, late = refs[:-2], refs[-2], refs[-1]
    chip = lax.axis_index("exp") // 2
    early[...] = jnp.concatenate([ref[chip ^ k] for ref in hidden for k in order[:-1]], axis=0)
    late[...] = jnp.concatenate([ref[chip ^ order[-1]] for ref in hidden], axis=0)


def weight_early_kernel(*refs):
    rows, units, out = refs[:-2], refs[-2], refs[-1]
    out[...] = lax.dot_general(
        jnp.concatenate([ref[...] for ref in rows], axis=0),
        units[...],
        (((0,), (0,)), ((), ())),
        preferred_element_type=jnp.float32,
    )


def finish_kernel(step, replicas, parts, *refs):
    rows = refs[:replicas]
    units, early, pulled, saved, _, out, grads, held, held_grads, sems = refs[replicas:]
    size = early.shape[0] // parts
    copies = []
    for i in range(parts):
        span = pl.ds(i * size, size)
        left = jnp.concatenate([ref[:, i * size : (i + 1) * size] for ref in rows], axis=0)
        held[span, :] = early[span, :] + lax.dot_general(
            left, units[...], (((0,), (0,)), ((), ())), preferred_element_type=jnp.float32
        )
        copies.append(pltpu.make_async_copy(held.at[span, :], out.at[0, span, :], sems.at[i]))
        copies[-1].start()
        if i == 0:
            place = (lax.axis_index("exp") // 2) ^ step
            held_grads[...] = pair_grads(pulled[...], saved[place])
            copies.append(pltpu.make_async_copy(held_grads, grads.at[place], sems.at[parts]))
            copies[-1].start()
    for copy in copies:
        copy.wait()


def token_kernel(same, other, last_slots, own, sib, weights, out):
    values = jnp.concatenate([same[...], other[...]], axis=1)
    hot = lax.broadcasted_iota(jnp.int32, (values.shape[1], out.shape[1]), 0) == last_slots[...]
    found = lax.dot_general(
        jnp.broadcast_to(values, (8, values.shape[1])),
        hot.astype(jnp.float32),
        (((1,), (0,)), ((), ())),
        precision=lax.Precision.HIGHEST,
        preferred_element_type=jnp.float32,
    )[0:1]
    weight = weights[...].astype(jnp.bfloat16).astype(jnp.float32)
    out[...] = (own[...] + sib[...] + found) / weight


def shards(cotangent, routes, gate_weight, down_weight, saved_pre):
    peers = lax.axis_size("exp")
    replicas = lax.axis_size("rep")
    rows_all = saved_pre.shape[2]
    cap = rows_all // peers
    chips = peers // 2
    pair = 2 * cap
    if pair % 16:
        return plain_shards(cotangent, routes, gate_weight, down_weight, saved_pre)
    width = down_weight.shape[2]
    tokens, model = cotangent.shape
    share = model // replicas

    last = chips // 2
    early = [k for k in range(chips) if k != last]
    order = early + [last]

    routes = routes.reshape(1, tokens)
    weights = gate_weight.reshape(1, tokens)
    cot_sib = swap(cotangent, "exp", 1)
    routes_sib = swap(routes, "exp", 1)
    weights_sib = swap(weights, "exp", 1)
    own_rows = kernel_call(
        copy_kernel,
        [jax.ShapeDtypeStruct((tokens, model), jnp.bfloat16)],
        [cotangent],
        "own_rows",
        LARGE,
    )[0]
    *blocks, slots, last_slots = kernel_call(
        lambda *refs: place_kernel(cap, order, *refs),
        [jax.ShapeDtypeStruct((replicas, pair, share), jnp.bfloat16)] * chips
        + [
            jax.ShapeDtypeStruct((2, tokens), jnp.int32),
            jax.ShapeDtypeStruct((1, tokens), jnp.int32),
        ],
        [own_rows, cot_sib, routes, routes_sib, weights, weights_sib],
        "place",
    )

    blocks = dict(zip(order, blocks))
    arrived = {0: blocks[0]}
    for k in early[1:]:
        arrived[k] = swap(blocks[k], "exp", 2 * k)
    saved = saved_pre.reshape(chips, pair, 2 * width)
    saved, slots = lax.optimization_barrier((saved, slots))
    hidden = kernel_call(
        hidden_kernel,
        [jax.ShapeDtypeStruct((chips, pair, width), jnp.bfloat16)],
        [saved],
        "hidden",
    )[0]
    hidden_of = [hidden] + [swap(hidden, "rep", j) for j in range(1, replicas)]
    units, units_last = kernel_call(
        lambda *refs: units_kernel(order, *refs),
        [
            jax.ShapeDtypeStruct((replicas * len(early) * pair, width), jnp.bfloat16),
            jax.ShapeDtypeStruct((replicas * pair, width), jnp.bfloat16),
        ],
        hidden_of,
        "units",
    )

    rows, last_block, units = lax.optimization_barrier(
        ([arrived[k] for k in reversed(early)], blocks[last], units)
    )
    arrived = dict(zip(reversed(early), rows))
    last_rows = swap(last_block, "exp", 2 * last)
    early_rows = stack([arrived[k] for k in early])
    early_rows = [early_rows[0]] + [swap(early_rows[j], "rep", j) for j in range(1, replicas)]
    grads, *routers = kernel_call(
        lambda *refs: pull_early_kernel(early, *refs),
        [jax.ShapeDtypeStruct(saved.shape, jnp.bfloat16)]
        + [jax.ShapeDtypeStruct((1, pair), jnp.float32)] * len(early),
        [*[arrived[k] for k in early], down_weight, saved],
        "pull_early",
    )
    returned = routers[:1] + [swap(router, "exp", 2 * k) for router, k in zip(routers[1:], early[1:])]
    total = kernel_call(
        weight_early_kernel,
        [jax.ShapeDtypeStruct((share, width), jnp.float32)],
        [*early_rows, units],
        "weight_early",
    )[0]

    rows, grads, total, returned = lax.optimization_barrier((last_rows, grads, total, returned))
    late_rows = [rows[0]] + [swap(rows[j], "rep", j) for j in range(1, replicas)]
    pulled, *routers = kernel_call(
        lambda *refs: pull_last_kernel(last, *refs),
        [jax.ShapeDtypeStruct((pair, width), jnp.float32)]
        + [jax.ShapeDtypeStruct((1, cap), jnp.float32)] * 2,
        [rows, down_weight, saved],
        "pull_last",
    )
    returned = jnp.concatenate(returned, axis=1).reshape(len(early) * pair, 1)
    slot_index = lax.broadcasted_iota(jnp.int32, (len(early) * pair, 1), 0)
    sums = [
        jnp.sum(jnp.where(slot_index == ids, returned, 0.0), axis=0, keepdims=True)
        for ids in (slots[0:1], slots[1:2])
    ]
    sum_sib = swap(sums[1], "exp", 1)
    routers, sum_sib = lax.optimization_barrier((routers, sum_sib))
    returned_last = [swap(routers[i], "exp", 2 * last + i) for i in range(2)]
    parts = 8
    weight_grad, grads = kernel_call(
        lambda *refs: finish_kernel(last, replicas, parts, *refs),
        [
            jax.ShapeDtypeStruct((1, share, width), jnp.float32),
            jax.ShapeDtypeStruct(saved.shape, jnp.bfloat16),
        ],
        [*late_rows, units_last, total, pulled, saved, grads],
        "finish",
        LARGE,
        in_specs=[WHOLE_VMEM] * (replicas + 4) + [IN_PLACE],
        out_specs=[IN_PLACE] * 2,
        input_output_aliases={replicas + 4: 1},
        scratch_shapes=[
            pltpu.VMEM((share, width), jnp.float32),
            pltpu.VMEM((pair, 2 * width), jnp.bfloat16),
            pltpu.SemaphoreType.DMA((parts + 1,)),
        ],
    )
    returned_last, weight_grad = lax.optimization_barrier((returned_last, weight_grad))
    token_grad = kernel_call(
        token_kernel,
        [jax.ShapeDtypeStruct((1, tokens), jnp.float32)],
        [*returned_last, last_slots, sums[0], sum_sib, weights],
        "token",
    )[0]
    return (weight_grad, grads.reshape(1, 1, rows_all, 2 * width), token_grad.reshape(tokens, 1))


def plain_shards(cotangent, routes, gate_weight, down_weight, saved_pre):
    peers = lax.axis_size("exp")
    replicas = lax.axis_size("rep")
    me = lax.axis_index("exp")
    mine = lax.axis_index("rep")
    rows_all = saved_pre.shape[2]
    capacity = rows_all // peers
    width = down_weight.shape[2]
    model = cotangent.shape[1]
    share = model // replicas

    expert_ids = routes[:, 0]
    experts = lax.broadcasted_iota(jnp.int32, (1, peers), 1)
    one_hot = (expert_ids[:, None] == experts).astype(jnp.int32)
    earlier = jnp.cumsum(one_hot, axis=0) - one_hot
    position = jnp.sum(earlier * one_hot, axis=1)
    slot_ids = (expert_ids ^ me) * capacity + position
    slot_index = lax.broadcasted_iota(jnp.int32, (rows_all, 1), 0)
    placement = slot_index == slot_ids[None, :]
    weight = gate_weight[:, 0].astype(jnp.bfloat16)
    outgoing = jnp.dot(
        jnp.where(placement, weight[None, :], 0), cotangent, preferred_element_type=jnp.float32
    ).astype(jnp.bfloat16)
    outgoing = outgoing.reshape(peers, capacity, model)

    groups = [
        list(range(0, peers // 2)),
        list(range(peers // 2, peers // 4 * 3)),
        list(range(peers // 4 * 3, peers)),
    ]
    arrived = {0: outgoing[0]}
    for k in groups[1] + groups[2] + groups[0][1:]:
        arrived[k] = swap(outgoing[k], "exp", k)

    saved = saved_pre[0, 0].reshape(peers, capacity, 2 * width)
    saved = jnp.take(saved, jnp.arange(peers) ^ me, axis=0).reshape(rows_all, 2 * width)
    saved = saved.astype(jnp.float32)
    gate_pre = saved[:, :width]
    up_pre = saved[:, width:]
    sigmoid_gate = jax.nn.sigmoid(gate_pre)
    silu_gate = gate_pre * sigmoid_gate
    hidden = silu_gate * up_pre
    hidden_sent = hidden.astype(jnp.bfloat16)
    hidden_of = [hidden_sent] + [swap(hidden_sent, "rep", j) for j in range(1, replicas)]
    gate_factor = up_pre * sigmoid_gate * (1.0 + gate_pre * (1.0 - sigmoid_gate))

    total = 0
    pulled_parts = []
    returned = []
    for group in groups:
        begin, end = group[0] * capacity, (group[-1] + 1) * capacity
        rows = jnp.concatenate([arrived[k] for k in group], axis=0)
        columns = [
            lax.dynamic_slice_in_dim(rows, (mine ^ j) * share, share, 1) for j in range(replicas)
        ]
        left = [columns[0]] + [swap(columns[j], "rep", j) for j in range(1, replicas)]
        right = [hidden_of[j][begin:end] for j in range(replicas)]
        total = total + lax.dot_general(
            jnp.concatenate(left, axis=0),
            jnp.concatenate(right, axis=0),
            (((0,), (0,)), ((), ())),
            preferred_element_type=jnp.float32,
        )
        pulled = jnp.dot(rows, down_weight[0], preferred_element_type=jnp.float32)
        pulled_parts.append(pulled)
        router = jnp.sum(pulled * hidden[begin:end], axis=1).reshape(len(group), capacity)
        returned += [router[i] if k == 0 else swap(router[i], "exp", k) for i, k in enumerate(group)]
    pulled = jnp.concatenate(pulled_parts, axis=0)
    pair_grads = jnp.concatenate([pulled * gate_factor, pulled * silu_gate], axis=1).astype(
        jnp.bfloat16
    )
    pair_grads = pair_grads.reshape(peers, capacity, 2 * width)
    pair_grads = jnp.take(pair_grads, jnp.arange(peers) ^ me, axis=0)
    returned_grad = jnp.concatenate(returned, axis=0)
    token_grad = jnp.sum(jnp.where(placement, returned_grad[:, None], 0.0), axis=0)
    token_grad = token_grad / weight.astype(jnp.float32)
    return (
        total[None],
        pair_grads.reshape(1, 1, rows_all, 2 * width),
        token_grad[:, None],
    )


def solution(mesh):
    in_specs = (
        P(("rep", "exp"), None),
        P(("rep", "exp"), None),
        P(("rep", "exp"), None),
        P("exp", None, None),
        P("rep", "exp", None, None),
    )
    out_specs = (P("exp", "rep", None), P("rep", "exp", None, None), P(("rep", "exp"), None))
    return jax.shard_map(shards, mesh=mesh, in_specs=in_specs, out_specs=out_specs, check_vma=False)
```

```python
import jax
import jax.numpy as jnp
from jax import lax
from jax.experimental import pallas as pl
from jax.experimental.pallas import tpu as pltpu
from jax.sharding import PartitionSpec as P

WHOLE_VMEM = pl.BlockSpec(memory_space=pltpu.VMEM)
IN_PLACE = pl.BlockSpec(memory_space=pl.ANY)
SMALL = pl.CostEstimate(flops=1024, bytes_accessed=1024, transcendentals=0)
LARGE = pl.CostEstimate(flops=10**10, bytes_accessed=1024, transcendentals=0)


def swap(value, axis, step):
    n = lax.axis_size(axis)
    return lax.ppermute(value, axis, [(i, i ^ step) for i in range(n)])


def kernel_call(kernel, outs, operands, name, cost=SMALL, vmem=24, **more):
    more.setdefault("in_specs", [WHOLE_VMEM] * len(operands))
    more.setdefault("out_specs", [WHOLE_VMEM] * len(outs))
    return pl.pallas_call(
        kernel,
        out_shape=outs,
        compiler_params=pltpu.CompilerParams(vmem_limit_bytes=vmem * 1024 * 1024),
        cost_estimate=cost,
        name=name,
        **more,
    )(*operands)


def copy_kernel(rows, out):
    out[...] = rows[...]


def hidden_kernel(saved, hidden):
    for k in range(saved.shape[0]):
        gate, up, sigmoid = gate_parts(saved[k])
        hidden[k] = (gate * sigmoid * up).astype(jnp.bfloat16)


def place_kernel(cap, order, cot, cot_sib, routes, routes_sib, weights, weights_sib, *outs):
    chips = len(order)
    blocks, slots_out, last_out = outs[:chips], outs[chips], outs[chips + 1]
    me, mine = lax.axis_index("exp"), lax.axis_index("rep")
    chip, core = me // 2, lax.rem(me, 2)
    replicas, pair, share = blocks[0].shape
    tokens = cot.shape[0]
    before = (
        lax.broadcasted_iota(jnp.int32, (tokens, tokens), 0)
        < lax.broadcasted_iota(jnp.int32, (tokens, tokens), 1)
    ).astype(jnp.bfloat16)
    placements = []
    for i, (ids, gains) in enumerate(((routes, weights), (routes_sib, weights_sib))):
        expert = ids[...]
        weight = gains[...].astype(jnp.bfloat16).astype(jnp.float32)
        hot = lax.broadcasted_iota(jnp.int32, (2 * chips, tokens), 0) == expert
        earlier = jnp.dot(hot.astype(jnp.bfloat16), before, preferred_element_type=jnp.float32)
        position = jnp.sum(jnp.where(hot, earlier, 0.0), axis=0, keepdims=True).astype(jnp.int32)
        source = core if i == 0 else 1 - core
        step = (expert >> 1) ^ chip
        same = (expert & 1) == core
        rank = sum(jnp.where(step == k, i, 0) for i, k in enumerate(order))
        slot = jnp.where(same, rank * pair + source * cap + position, -1)
        slots_out[i : i + 1, :] = slot
        if i == 0:
            last_out[...] = jnp.where(
                step == order[-1], jnp.where(same, position, cap + position), -1
            )
        here = lax.broadcasted_iota(jnp.int32, (chips * pair, tokens), 0) == slot
        placements.append(jnp.where(here, weight, 0.0).astype(jnp.bfloat16))
    placement = jnp.concatenate(placements, axis=1)
    for j in range(replicas):
        columns = pl.ds(pl.multiple_of((mine ^ j) * share, share), share)
        rows = jnp.concatenate([cot[:, columns], cot_sib[:, columns]], axis=0)
        sent = jnp.dot(placement, rows, preferred_element_type=jnp.float32).astype(jnp.bfloat16)
        for k in range(chips):
            blocks[k][j] = sent[k * pair : (k + 1) * pair]


def products(arrived, down):
    mine = lax.axis_index("rep")
    replicas, _, share = arrived[0].shape
    pulled = 0
    for j in range(replicas):
        rows = jnp.concatenate([ref[j] for ref in arrived], axis=0)
        begin = pl.multiple_of((mine ^ j) * share, share)
        pulled += jnp.dot(rows, down[0, pl.ds(begin, share), :], preferred_element_type=jnp.float32)
    return pulled


def gate_parts(saved):
    width = saved.shape[1] // 2
    gate, up = saved[:, :width].astype(jnp.float32), saved[:, width:].astype(jnp.float32)
    sigmoid = 1.0 / (1.0 + jnp.exp(-gate))
    return gate, up, sigmoid


def router_sums(pulled, saved):
    gate, up, sigmoid = gate_parts(saved)
    return lax.dot_general(
        jnp.ones((8, pulled.shape[1]), jnp.float32),
        pulled * (gate * sigmoid * up),
        (((1,), (1,)), ((), ())),
        precision=lax.Precision.HIGHEST,
        preferred_element_type=jnp.float32,
    )[0:1]


def pair_grads(pulled, saved):
    gate, up, sigmoid = gate_parts(saved)
    both = [pulled * up * sigmoid * (1.0 + gate * (1.0 - sigmoid)), pulled * (gate * sigmoid)]
    return jnp.concatenate(both, axis=1).astype(jnp.bfloat16)


def pull_early_kernel(steps, *refs):
    count = len(steps)
    arrived, (down, saved, grads), routers = refs[:count], refs[count : count + 3], refs[count + 3 :]
    chip = lax.axis_index("exp") // 2
    pulled = products(arrived, down)
    pair = arrived[0].shape[1]
    for i, k in enumerate(steps):
        part = pulled[i * pair : (i + 1) * pair]
        routers[i][...] = router_sums(part, saved[chip ^ k])
        grads[chip ^ k] = pair_grads(part, saved[chip ^ k])


def pull_last_kernel(step, arrived, down, saved, pulled, same, other):
    me = lax.axis_index("exp")
    chip, core = me // 2, lax.rem(me, 2)
    pulled[...] = products([arrived], down)
    router = router_sums(pulled[...], saved[chip ^ step])
    cap = router.shape[1] // 2
    same[...] = jnp.where(core == 0, router[:, :cap], router[:, cap:])
    other[...] = jnp.where(core == 0, router[:, cap:], router[:, :cap])


def stack_kernel(count, *refs):
    for j, out in enumerate(refs[count:]):
        out[...] = jnp.concatenate([ref[j] for ref in refs[:count]], axis=0)


def stack(rows):
    replicas, pair, share = rows[0].shape
    return kernel_call(
        lambda *refs: stack_kernel(len(rows), *refs),
        [jax.ShapeDtypeStruct((len(rows) * pair, share), jnp.bfloat16)] * replicas,
        rows,
        "stack",
    )


def units_kernel(order, *refs):
    hidden, early, late = refs[:-2], refs[-2], refs[-1]
    chip = lax.axis_index("exp") // 2
    early[...] = jnp.concatenate([ref[chip ^ k] for ref in hidden for k in order[:-1]], axis=0)
    late[...] = jnp.concatenate([ref[chip ^ order[-1]] for ref in hidden], axis=0)


def weight_early_kernel(*refs):
    rows, units, out = refs[:-2], refs[-2], refs[-1]
    out[...] = lax.dot_general(
        jnp.concatenate([ref[...] for ref in rows], axis=0),
        units[...],
        (((0,), (0,)), ((), ())),
        preferred_element_type=jnp.float32,
    )


def finish_kernel(step, replicas, parts, *refs):
    rows = refs[:replicas]
    units, early, pulled, saved, _, out, grads, held, held_grads, sems = refs[replicas:]
    size = early.shape[0] // parts
    copies = []
    for i in range(parts):
        span = pl.ds(i * size, size)
        left = jnp.concatenate([ref[:, i * size : (i + 1) * size] for ref in rows], axis=0)
        held[span, :] = early[span, :] + lax.dot_general(
            left, units[...], (((0,), (0,)), ((), ())), preferred_element_type=jnp.float32
        )
        copies.append(pltpu.make_async_copy(held.at[span, :], out.at[0, span, :], sems.at[i]))
        copies[-1].start()
        if i == 0:
            place = (lax.axis_index("exp") // 2) ^ step
            held_grads[...] = pair_grads(pulled[...], saved[place])
            copies.append(pltpu.make_async_copy(held_grads, grads.at[place], sems.at[parts]))
            copies[-1].start()
    for copy in copies:
        copy.wait()


def token_kernel(same, other, last_slots, own, sib, weights, out):
    values = jnp.concatenate([same[...], other[...]], axis=1)
    hot = lax.broadcasted_iota(jnp.int32, (values.shape[1], out.shape[1]), 0) == last_slots[...]
    found = lax.dot_general(
        jnp.broadcast_to(values, (8, values.shape[1])),
        hot.astype(jnp.float32),
        (((1,), (0,)), ((), ())),
        precision=lax.Precision.HIGHEST,
        preferred_element_type=jnp.float32,
    )[0:1]
    weight = weights[...].astype(jnp.bfloat16).astype(jnp.float32)
    out[...] = (own[...] + sib[...] + found) / weight


def shards(cotangent, routes, gate_weight, down_weight, saved_pre):
    peers = lax.axis_size("exp")
    replicas = lax.axis_size("rep")
    rows_all = saved_pre.shape[2]
    cap = rows_all // peers
    chips = peers // 2
    pair = 2 * cap
    if pair % 16:
        return plain_shards(cotangent, routes, gate_weight, down_weight, saved_pre)
    width = down_weight.shape[2]
    tokens, model = cotangent.shape
    share = model // replicas

    last = chips // 2
    early = [k for k in range(chips) if k != last]
    order = early + [last]

    routes = routes.reshape(1, tokens)
    weights = gate_weight.reshape(1, tokens)
    cot_sib = swap(cotangent, "exp", 1)
    routes_sib = swap(routes, "exp", 1)
    weights_sib = swap(weights, "exp", 1)
    own_rows = kernel_call(
        copy_kernel,
        [jax.ShapeDtypeStruct((tokens, model), jnp.bfloat16)],
        [cotangent],
        "own_rows",
        LARGE,
    )[0]
    *blocks, slots, last_slots = kernel_call(
        lambda *refs: place_kernel(cap, order, *refs),
        [jax.ShapeDtypeStruct((replicas, pair, share), jnp.bfloat16)] * chips
        + [
            jax.ShapeDtypeStruct((2, tokens), jnp.int32),
            jax.ShapeDtypeStruct((1, tokens), jnp.int32),
        ],
        [own_rows, cot_sib, routes, routes_sib, weights, weights_sib],
        "place",
    )

    blocks = dict(zip(order, blocks))
    arrived = {0: blocks[0]}
    for k in reversed(early[1:]):
        arrived[k] = swap(blocks[k], "exp", 2 * k)
    saved = saved_pre.reshape(chips, pair, 2 * width)
    saved, slots = lax.optimization_barrier((saved, slots))
    hidden = kernel_call(
        hidden_kernel,
        [jax.ShapeDtypeStruct((chips, pair, width), jnp.bfloat16)],
        [saved],
        "hidden",
    )[0]
    hidden_of = [hidden] + [swap(hidden, "rep", j) for j in range(1, replicas)]
    units, units_last = kernel_call(
        lambda *refs: units_kernel(order, *refs),
        [
            jax.ShapeDtypeStruct((replicas * len(early) * pair, width), jnp.bfloat16),
            jax.ShapeDtypeStruct((replicas * pair, width), jnp.bfloat16),
        ],
        hidden_of,
        "units",
    )

    rows, last_block, units = lax.optimization_barrier(
        ([arrived[k] for k in early], blocks[last], units)
    )
    arrived = dict(zip(early, rows))
    last_rows = swap(last_block, "exp", 2 * last)
    early_rows = stack(rows)
    early_rows = [early_rows[0]] + [swap(early_rows[j], "rep", j) for j in range(1, replicas)]
    grads, *routers = kernel_call(
        lambda *refs: pull_early_kernel(early, *refs),
        [jax.ShapeDtypeStruct(saved.shape, jnp.bfloat16)]
        + [jax.ShapeDtypeStruct((1, pair), jnp.float32)] * len(early),
        [*[arrived[k] for k in early], down_weight, saved],
        "pull_early",
    )
    returned = routers[:1] + [swap(router, "exp", 2 * k) for router, k in zip(routers[1:], early[1:])]
    total = kernel_call(
        weight_early_kernel,
        [jax.ShapeDtypeStruct((share, width), jnp.float32)],
        [*early_rows, units],
        "weight_early",
    )[0]

    rows, grads, total, near_returned = lax.optimization_barrier(
        (last_rows, grads, total, returned[:2])
    )
    returned = [*near_returned, *returned[2:]]
    late_rows = [rows[0]] + [swap(rows[j], "rep", j) for j in range(1, replicas)]
    pulled, *routers = kernel_call(
        lambda *refs: pull_last_kernel(last, *refs),
        [jax.ShapeDtypeStruct((pair, width), jnp.float32)]
        + [jax.ShapeDtypeStruct((1, cap), jnp.float32)] * 2,
        [rows, down_weight, saved],
        "pull_last",
    )
    returned = jnp.concatenate(returned, axis=1).reshape(len(early) * pair, 1)
    slot_index = lax.broadcasted_iota(jnp.int32, (len(early) * pair, 1), 0)
    sums = [
        jnp.sum(jnp.where(slot_index == ids, returned, 0.0), axis=0, keepdims=True)
        for ids in (slots[0:1], slots[1:2])
    ]
    sum_sib = swap(sums[1], "exp", 1)
    routers, sum_sib = lax.optimization_barrier((routers, sum_sib))
    returned_last = [swap(routers[i], "exp", 2 * last + i) for i in range(2)]
    parts = 4
    weight_grad, grads = kernel_call(
        lambda *refs: finish_kernel(last, replicas, parts, *refs),
        [
            jax.ShapeDtypeStruct((1, share, width), jnp.float32),
            jax.ShapeDtypeStruct(saved.shape, jnp.bfloat16),
        ],
        [*late_rows, units_last, total, pulled, saved, grads],
        "finish",
        LARGE,
        in_specs=[WHOLE_VMEM] * (replicas + 4) + [IN_PLACE],
        out_specs=[IN_PLACE] * 2,
        input_output_aliases={replicas + 4: 1},
        scratch_shapes=[
            pltpu.VMEM((share, width), jnp.float32),
            pltpu.VMEM((pair, 2 * width), jnp.bfloat16),
            pltpu.SemaphoreType.DMA((parts + 1,)),
        ],
    )
    returned_last, weight_grad = lax.optimization_barrier((returned_last, weight_grad))
    token_grad = kernel_call(
        token_kernel,
        [jax.ShapeDtypeStruct((1, tokens), jnp.float32)],
        [*returned_last, last_slots, sums[0], sum_sib, weights],
        "token",
    )[0]
    return (weight_grad, grads.reshape(1, 1, rows_all, 2 * width), token_grad.reshape(tokens, 1))


def plain_shards(cotangent, routes, gate_weight, down_weight, saved_pre):
    peers = lax.axis_size("exp")
    replicas = lax.axis_size("rep")
    me = lax.axis_index("exp")
    mine = lax.axis_index("rep")
    rows_all = saved_pre.shape[2]
    capacity = rows_all // peers
    width = down_weight.shape[2]
    model = cotangent.shape[1]
    share = model // replicas

    expert_ids = routes[:, 0]
    experts = lax.broadcasted_iota(jnp.int32, (1, peers), 1)
    one_hot = (expert_ids[:, None] == experts).astype(jnp.int32)
    earlier = jnp.cumsum(one_hot, axis=0) - one_hot
    position = jnp.sum(earlier * one_hot, axis=1)
    slot_ids = (expert_ids ^ me) * capacity + position
    slot_index = lax.broadcasted_iota(jnp.int32, (rows_all, 1), 0)
    placement = slot_index == slot_ids[None, :]
    weight = gate_weight[:, 0].astype(jnp.bfloat16)
    outgoing = jnp.dot(
        jnp.where(placement, weight[None, :], 0), cotangent, preferred_element_type=jnp.float32
    ).astype(jnp.bfloat16)
    outgoing = outgoing.reshape(peers, capacity, model)

    groups = [
        list(range(0, peers // 2)),
        list(range(peers // 2, peers // 4 * 3)),
        list(range(peers // 4 * 3, peers)),
    ]
    arrived = {0: outgoing[0]}
    for k in groups[1] + groups[2] + groups[0][1:]:
        arrived[k] = swap(outgoing[k], "exp", k)

    saved = saved_pre[0, 0].reshape(peers, capacity, 2 * width)
    saved = jnp.take(saved, jnp.arange(peers) ^ me, axis=0).reshape(rows_all, 2 * width)
    saved = saved.astype(jnp.float32)
    gate_pre = saved[:, :width]
    up_pre = saved[:, width:]
    sigmoid_gate = jax.nn.sigmoid(gate_pre)
    silu_gate = gate_pre * sigmoid_gate
    hidden = silu_gate * up_pre
    hidden_sent = hidden.astype(jnp.bfloat16)
    hidden_of = [hidden_sent] + [swap(hidden_sent, "rep", j) for j in range(1, replicas)]
    gate_factor = up_pre * sigmoid_gate * (1.0 + gate_pre * (1.0 - sigmoid_gate))

    total = 0
    pulled_parts = []
    returned = []
    for group in groups:
        begin, end = group[0] * capacity, (group[-1] + 1) * capacity
        rows = jnp.concatenate([arrived[k] for k in group], axis=0)
        columns = [
            lax.dynamic_slice_in_dim(rows, (mine ^ j) * share, share, 1) for j in range(replicas)
        ]
        left = [columns[0]] + [swap(columns[j], "rep", j) for j in range(1, replicas)]
        right = [hidden_of[j][begin:end] for j in range(replicas)]
        total = total + lax.dot_general(
            jnp.concatenate(left, axis=0),
            jnp.concatenate(right, axis=0),
            (((0,), (0,)), ((), ())),
            preferred_element_type=jnp.float32,
        )
        pulled = jnp.dot(rows, down_weight[0], preferred_element_type=jnp.float32)
        pulled_parts.append(pulled)
        router = jnp.sum(pulled * hidden[begin:end], axis=1).reshape(len(group), capacity)
        returned += [router[i] if k == 0 else swap(router[i], "exp", k) for i, k in enumerate(group)]
    pulled = jnp.concatenate(pulled_parts, axis=0)
    pair_grads = jnp.concatenate([pulled * gate_factor, pulled * silu_gate], axis=1).astype(
        jnp.bfloat16
    )
    pair_grads = pair_grads.reshape(peers, capacity, 2 * width)
    pair_grads = jnp.take(pair_grads, jnp.arange(peers) ^ me, axis=0)
    returned_grad = jnp.concatenate(returned, axis=0)
    token_grad = jnp.sum(jnp.where(placement, returned_grad[:, None], 0.0), axis=0)
    token_grad = token_grad / weight.astype(jnp.float32)
    return (
        total[None],
        pair_grads.reshape(1, 1, rows_all, 2 * width),
        token_grad[:, None],
    )


def solution(mesh):
    in_specs = (
        P(("rep", "exp"), None),
        P(("rep", "exp"), None),
        P(("rep", "exp"), None),
        P("exp", None, None),
        P("rep", "exp", None, None),
    )
    out_specs = (P("exp", "rep", None), P("rep", "exp", None, None), P(("rep", "exp"), None))
    return jax.shard_map(shards, mesh=mesh, in_specs=in_specs, out_specs=out_specs, check_vma=False)
```

```python
import jax
import jax.numpy as jnp
from jax import lax
from jax.experimental import pallas as pl
from jax.experimental.pallas import tpu as pltpu
from jax.sharding import PartitionSpec as P

WHOLE_VMEM = pl.BlockSpec(memory_space=pltpu.VMEM)
IN_PLACE = pl.BlockSpec(memory_space=pl.ANY)
SMALL = pl.CostEstimate(flops=1024, bytes_accessed=1024, transcendentals=0)
LARGE = pl.CostEstimate(flops=10**10, bytes_accessed=1024, transcendentals=0)


def swap(value, axis, step):
    n = lax.axis_size(axis)
    return lax.ppermute(value, axis, [(i, i ^ step) for i in range(n)])


def kernel_call(kernel, outs, operands, name, cost=SMALL, vmem=24, **more):
    more.setdefault("in_specs", [WHOLE_VMEM] * len(operands))
    more.setdefault("out_specs", [WHOLE_VMEM] * len(outs))
    return pl.pallas_call(
        kernel,
        out_shape=outs,
        compiler_params=pltpu.CompilerParams(vmem_limit_bytes=vmem * 1024 * 1024),
        cost_estimate=cost,
        name=name,
        **more,
    )(*operands)


def copy_kernel(rows, out):
    out[...] = rows[...]


def hidden_kernel(saved, hidden):
    for k in range(saved.shape[0]):
        gate, up, sigmoid = gate_parts(saved[k])
        hidden[k] = (gate * sigmoid * up).astype(jnp.bfloat16)


def placement_of(cap, order, own, ids, gains):
    me = lax.axis_index("exp")
    chip, core = me // 2, lax.rem(me, 2)
    source = core if own else 1 - core
    chips, pair, tokens = len(order), 2 * cap, ids.shape[1]
    before = (
        lax.broadcasted_iota(jnp.int32, (tokens, tokens), 0)
        < lax.broadcasted_iota(jnp.int32, (tokens, tokens), 1)
    ).astype(jnp.bfloat16)
    expert = ids[...]
    weight = gains[...].astype(jnp.bfloat16).astype(jnp.float32)
    hot = lax.broadcasted_iota(jnp.int32, (2 * chips, tokens), 0) == expert
    earlier = jnp.dot(hot.astype(jnp.bfloat16), before, preferred_element_type=jnp.float32)
    position = jnp.sum(jnp.where(hot, earlier, 0.0), axis=0, keepdims=True).astype(jnp.int32)
    step = (expert >> 1) ^ chip
    same = (expert & 1) == core
    rank = sum(jnp.where(step == k, i, 0) for i, k in enumerate(order))
    slot = jnp.where(same, rank * pair + source * cap + position, -1)
    last_slot = jnp.where(step == order[-1], jnp.where(same, position, cap + position), -1)
    here = lax.broadcasted_iota(jnp.int32, (chips * pair, tokens), 0) == slot
    return slot, last_slot, jnp.where(here, weight, 0.0).astype(jnp.bfloat16)


def place_own_kernel(cap, order, cot, ids, gains, placed, slots, last_slots):
    mine = lax.axis_index("rep")
    replicas, _, share = placed.shape
    slots[...], last_slots[...], placement = placement_of(cap, order, True, ids, gains)
    for j in range(replicas):
        columns = pl.ds(pl.multiple_of((mine ^ j) * share, share), share)
        placed[j] = jnp.dot(
            placement, cot[:, columns], preferred_element_type=jnp.float32
        ).astype(jnp.bfloat16)


def place_sib_kernel(cap, order, placed, cot, ids, gains, *outs):
    mine = lax.axis_index("rep")
    blocks, slots = outs[:-1], outs[-1]
    replicas, pair, share = blocks[0].shape
    slots[...], _, placement = placement_of(cap, order, False, ids, gains)
    for j in range(replicas):
        columns = pl.ds(pl.multiple_of((mine ^ j) * share, share), share)
        sent = jnp.dot(placement, cot[:, columns], preferred_element_type=jnp.float32)
        sent = (sent + placed[j].astype(jnp.float32)).astype(jnp.bfloat16)
        for i, block in enumerate(blocks):
            block[j] = sent[i * pair : (i + 1) * pair]


def products(arrived, down):
    mine = lax.axis_index("rep")
    replicas, _, share = arrived[0].shape
    pulled = 0
    for j in range(replicas):
        rows = jnp.concatenate([ref[j] for ref in arrived], axis=0)
        begin = pl.multiple_of((mine ^ j) * share, share)
        pulled += jnp.dot(rows, down[0, pl.ds(begin, share), :], preferred_element_type=jnp.float32)
    return pulled


def gate_parts(saved):
    width = saved.shape[1] // 2
    gate, up = saved[:, :width].astype(jnp.float32), saved[:, width:].astype(jnp.float32)
    sigmoid = 1.0 / (1.0 + jnp.exp(-gate))
    return gate, up, sigmoid


def router_sums(pulled, saved):
    gate, up, sigmoid = gate_parts(saved)
    return lax.dot_general(
        jnp.ones((8, pulled.shape[1]), jnp.float32),
        pulled * (gate * sigmoid * up),
        (((1,), (1,)), ((), ())),
        precision=lax.Precision.HIGHEST,
        preferred_element_type=jnp.float32,
    )[0:1]


def pair_grads(pulled, saved):
    gate, up, sigmoid = gate_parts(saved)
    both = [pulled * up * sigmoid * (1.0 + gate * (1.0 - sigmoid)), pulled * (gate * sigmoid)]
    return jnp.concatenate(both, axis=1).astype(jnp.bfloat16)


def pull_early_kernel(steps, *refs):
    count = len(steps)
    arrived, (down, saved, grads), routers = refs[:count], refs[count : count + 3], refs[count + 3 :]
    chip = lax.axis_index("exp") // 2
    pulled = products(arrived, down)
    pair = arrived[0].shape[1]
    for i, k in enumerate(steps):
        part = pulled[i * pair : (i + 1) * pair]
        routers[i][...] = router_sums(part, saved[chip ^ k])
        grads[chip ^ k] = pair_grads(part, saved[chip ^ k])


def pull_last_kernel(step, arrived, down, saved, pulled, same, other):
    me = lax.axis_index("exp")
    chip, core = me // 2, lax.rem(me, 2)
    pulled[...] = products([arrived], down)
    router = router_sums(pulled[...], saved[chip ^ step])
    cap = router.shape[1] // 2
    same[...] = jnp.where(core == 0, router[:, :cap], router[:, cap:])
    other[...] = jnp.where(core == 0, router[:, cap:], router[:, :cap])


def stack_kernel(count, *refs):
    for j, out in enumerate(refs[count:]):
        out[...] = jnp.concatenate([ref[j] for ref in refs[:count]], axis=0)


def stack(rows):
    replicas, pair, share = rows[0].shape
    return kernel_call(
        lambda *refs: stack_kernel(len(rows), *refs),
        [jax.ShapeDtypeStruct((len(rows) * pair, share), jnp.bfloat16)] * replicas,
        rows,
        "stack",
    )


def units_kernel(order, *refs):
    hidden, early, late = refs[:-2], refs[-2], refs[-1]
    chip = lax.axis_index("exp") // 2
    early[...] = jnp.concatenate([ref[chip ^ k] for ref in hidden for k in order[:-1]], axis=0)
    late[...] = jnp.concatenate([ref[chip ^ order[-1]] for ref in hidden], axis=0)


def weight_early_kernel(*refs):
    rows, units, out = refs[:-2], refs[-2], refs[-1]
    out[...] = lax.dot_general(
        jnp.concatenate([ref[...] for ref in rows], axis=0),
        units[...],
        (((0,), (0,)), ((), ())),
        preferred_element_type=jnp.float32,
    )


def finish_kernel(step, replicas, parts, *refs):
    rows = refs[:replicas]
    units, early, pulled, saved, _, out, grads, held, held_grads, sems = refs[replicas:]
    size = early.shape[0] // parts
    copies = []
    for i in range(parts):
        span = pl.ds(i * size, size)
        left = jnp.concatenate([ref[:, i * size : (i + 1) * size] for ref in rows], axis=0)
        held[span, :] = early[span, :] + lax.dot_general(
            left, units[...], (((0,), (0,)), ((), ())), preferred_element_type=jnp.float32
        )
        copies.append(pltpu.make_async_copy(held.at[span, :], out.at[0, span, :], sems.at[i]))
        copies[-1].start()
        if i == 0:
            place = (lax.axis_index("exp") // 2) ^ step
            held_grads[...] = pair_grads(pulled[...], saved[place])
            copies.append(pltpu.make_async_copy(held_grads, grads.at[place], sems.at[parts]))
            copies[-1].start()
    for copy in copies:
        copy.wait()


def token_kernel(same, other, last_slots, own, sib, weights, out):
    values = jnp.concatenate([same[...], other[...]], axis=1)
    hot = lax.broadcasted_iota(jnp.int32, (values.shape[1], out.shape[1]), 0) == last_slots[...]
    found = lax.dot_general(
        jnp.broadcast_to(values, (8, values.shape[1])),
        hot.astype(jnp.float32),
        (((1,), (0,)), ((), ())),
        precision=lax.Precision.HIGHEST,
        preferred_element_type=jnp.float32,
    )[0:1]
    weight = weights[...].astype(jnp.bfloat16).astype(jnp.float32)
    out[...] = (own[...] + sib[...] + found) / weight


def shards(cotangent, routes, gate_weight, down_weight, saved_pre):
    peers = lax.axis_size("exp")
    replicas = lax.axis_size("rep")
    rows_all = saved_pre.shape[2]
    cap = rows_all // peers
    chips = peers // 2
    pair = 2 * cap
    if pair % 16:
        return plain_shards(cotangent, routes, gate_weight, down_weight, saved_pre)
    width = down_weight.shape[2]
    tokens, model = cotangent.shape
    share = model // replicas

    last = chips // 2
    early = [k for k in range(chips) if k != last]
    order = early + [last]

    routes = routes.reshape(1, tokens)
    weights = gate_weight.reshape(1, tokens)
    cot_sib = swap(cotangent, "exp", 1)
    routes_sib = swap(routes, "exp", 1)
    weights_sib = swap(weights, "exp", 1)
    own_rows = kernel_call(
        copy_kernel,
        [jax.ShapeDtypeStruct((tokens, model), jnp.bfloat16)],
        [cotangent],
        "own_rows",
        LARGE,
    )[0]
    slot_shape = jax.ShapeDtypeStruct((1, tokens), jnp.int32)
    placed, slots, last_slots = kernel_call(
        lambda *refs: place_own_kernel(cap, order, *refs),
        [jax.ShapeDtypeStruct((replicas, chips * pair, share), jnp.bfloat16), slot_shape, slot_shape],
        [own_rows, routes, weights],
        "place_own",
    )
    *blocks, slots_sib = kernel_call(
        lambda *refs: place_sib_kernel(cap, order, *refs),
        [jax.ShapeDtypeStruct((replicas, pair, share), jnp.bfloat16)] * chips + [slot_shape],
        [placed, cot_sib, routes_sib, weights_sib],
        "place_sib",
    )

    blocks = dict(zip(order, blocks))
    arrived = {0: blocks[0]}
    for k in reversed(early[1:]):
        arrived[k] = swap(blocks[k], "exp", 2 * k)
    saved = saved_pre.reshape(chips, pair, 2 * width)
    saved, slots_sib = lax.optimization_barrier((saved, slots_sib))
    hidden = kernel_call(
        hidden_kernel,
        [jax.ShapeDtypeStruct((chips, pair, width), jnp.bfloat16)],
        [saved],
        "hidden",
    )[0]
    hidden_of = [hidden] + [swap(hidden, "rep", j) for j in range(1, replicas)]
    units, units_last = kernel_call(
        lambda *refs: units_kernel(order, *refs),
        [
            jax.ShapeDtypeStruct((replicas * len(early) * pair, width), jnp.bfloat16),
            jax.ShapeDtypeStruct((replicas * pair, width), jnp.bfloat16),
        ],
        hidden_of,
        "units",
    )

    rows, last_block, units = lax.optimization_barrier(
        ([arrived[k] for k in early], blocks[last], units)
    )
    arrived = dict(zip(early, rows))
    last_rows = swap(last_block, "exp", 2 * last)
    early_rows = stack(rows)
    early_rows = [early_rows[0]] + [swap(early_rows[j], "rep", j) for j in range(1, replicas)]
    grads, *routers = kernel_call(
        lambda *refs: pull_early_kernel(early, *refs),
        [jax.ShapeDtypeStruct(saved.shape, jnp.bfloat16)]
        + [jax.ShapeDtypeStruct((1, pair), jnp.float32)] * len(early),
        [*[arrived[k] for k in early], down_weight, saved],
        "pull_early",
    )
    returned = routers[:1] + [swap(router, "exp", 2 * k) for router, k in zip(routers[1:], early[1:])]
    total = kernel_call(
        weight_early_kernel,
        [jax.ShapeDtypeStruct((share, width), jnp.float32)],
        [*early_rows, units],
        "weight_early",
    )[0]

    rows, grads, total, returned = lax.optimization_barrier(
        (last_rows, grads, total, returned[::-1])
    )
    returned = returned[::-1]
    late_rows = [rows[0]] + [swap(rows[j], "rep", j) for j in range(1, replicas)]
    pulled, *routers = kernel_call(
        lambda *refs: pull_last_kernel(last, *refs),
        [jax.ShapeDtypeStruct((pair, width), jnp.float32)]
        + [jax.ShapeDtypeStruct((1, cap), jnp.float32)] * 2,
        [rows, down_weight, saved],
        "pull_last",
    )
    returned = jnp.concatenate(returned, axis=1).reshape(len(early) * pair, 1)
    slot_index = lax.broadcasted_iota(jnp.int32, (len(early) * pair, 1), 0)
    sums = [
        jnp.sum(jnp.where(slot_index == ids, returned, 0.0), axis=0, keepdims=True)
        for ids in (slots, slots_sib)
    ]
    sum_sib = swap(sums[1], "exp", 1)
    routers, sum_sib = lax.optimization_barrier((routers, sum_sib))
    returned_last = [swap(routers[i], "exp", 2 * last + i) for i in range(2)]
    parts = 4
    weight_grad, grads = kernel_call(
        lambda *refs: finish_kernel(last, replicas, parts, *refs),
        [
            jax.ShapeDtypeStruct((1, share, width), jnp.float32),
            jax.ShapeDtypeStruct(saved.shape, jnp.bfloat16),
        ],
        [*late_rows, units_last, total, pulled, saved, grads],
        "finish",
        LARGE,
        in_specs=[WHOLE_VMEM] * (replicas + 4) + [IN_PLACE],
        out_specs=[IN_PLACE] * 2,
        input_output_aliases={replicas + 4: 1},
        scratch_shapes=[
            pltpu.VMEM((share, width), jnp.float32),
            pltpu.VMEM((pair, 2 * width), jnp.bfloat16),
            pltpu.SemaphoreType.DMA((parts + 1,)),
        ],
    )
    returned_last, weight_grad = lax.optimization_barrier((returned_last, weight_grad))
    token_grad = kernel_call(
        token_kernel,
        [jax.ShapeDtypeStruct((1, tokens), jnp.float32)],
        [*returned_last, last_slots, sums[0], sum_sib, weights],
        "token",
    )[0]
    return (weight_grad, grads.reshape(1, 1, rows_all, 2 * width), token_grad.reshape(tokens, 1))


def plain_shards(cotangent, routes, gate_weight, down_weight, saved_pre):
    peers = lax.axis_size("exp")
    replicas = lax.axis_size("rep")
    me = lax.axis_index("exp")
    mine = lax.axis_index("rep")
    rows_all = saved_pre.shape[2]
    capacity = rows_all // peers
    width = down_weight.shape[2]
    model = cotangent.shape[1]
    share = model // replicas

    expert_ids = routes[:, 0]
    experts = lax.broadcasted_iota(jnp.int32, (1, peers), 1)
    one_hot = (expert_ids[:, None] == experts).astype(jnp.int32)
    earlier = jnp.cumsum(one_hot, axis=0) - one_hot
    position = jnp.sum(earlier * one_hot, axis=1)
    slot_ids = (expert_ids ^ me) * capacity + position
    slot_index = lax.broadcasted_iota(jnp.int32, (rows_all, 1), 0)
    placement = slot_index == slot_ids[None, :]
    weight = gate_weight[:, 0].astype(jnp.bfloat16)
    outgoing = jnp.dot(
        jnp.where(placement, weight[None, :], 0), cotangent, preferred_element_type=jnp.float32
    ).astype(jnp.bfloat16)
    outgoing = outgoing.reshape(peers, capacity, model)

    groups = [
        list(range(0, peers // 2)),
        list(range(peers // 2, peers // 4 * 3)),
        list(range(peers // 4 * 3, peers)),
    ]
    arrived = {0: outgoing[0]}
    for k in groups[1] + groups[2] + groups[0][1:]:
        arrived[k] = swap(outgoing[k], "exp", k)

    saved = saved_pre[0, 0].reshape(peers, capacity, 2 * width)
    saved = jnp.take(saved, jnp.arange(peers) ^ me, axis=0).reshape(rows_all, 2 * width)
    saved = saved.astype(jnp.float32)
    gate_pre = saved[:, :width]
    up_pre = saved[:, width:]
    sigmoid_gate = jax.nn.sigmoid(gate_pre)
    silu_gate = gate_pre * sigmoid_gate
    hidden = silu_gate * up_pre
    hidden_sent = hidden.astype(jnp.bfloat16)
    hidden_of = [hidden_sent] + [swap(hidden_sent, "rep", j) for j in range(1, replicas)]
    gate_factor = up_pre * sigmoid_gate * (1.0 + gate_pre * (1.0 - sigmoid_gate))

    total = 0
    pulled_parts = []
    returned = []
    for group in groups:
        begin, end = group[0] * capacity, (group[-1] + 1) * capacity
        rows = jnp.concatenate([arrived[k] for k in group], axis=0)
        columns = [
            lax.dynamic_slice_in_dim(rows, (mine ^ j) * share, share, 1) for j in range(replicas)
        ]
        left = [columns[0]] + [swap(columns[j], "rep", j) for j in range(1, replicas)]
        right = [hidden_of[j][begin:end] for j in range(replicas)]
        total = total + lax.dot_general(
            jnp.concatenate(left, axis=0),
            jnp.concatenate(right, axis=0),
            (((0,), (0,)), ((), ())),
            preferred_element_type=jnp.float32,
        )
        pulled = jnp.dot(rows, down_weight[0], preferred_element_type=jnp.float32)
        pulled_parts.append(pulled)
        router = jnp.sum(pulled * hidden[begin:end], axis=1).reshape(len(group), capacity)
        returned += [router[i] if k == 0 else swap(router[i], "exp", k) for i, k in enumerate(group)]
    pulled = jnp.concatenate(pulled_parts, axis=0)
    pair_grads = jnp.concatenate([pulled * gate_factor, pulled * silu_gate], axis=1).astype(
        jnp.bfloat16
    )
    pair_grads = pair_grads.reshape(peers, capacity, 2 * width)
    pair_grads = jnp.take(pair_grads, jnp.arange(peers) ^ me, axis=0)
    returned_grad = jnp.concatenate(returned, axis=0)
    token_grad = jnp.sum(jnp.where(placement, returned_grad[:, None], 0.0), axis=0)
    token_grad = token_grad / weight.astype(jnp.float32)
    return (
        total[None],
        pair_grads.reshape(1, 1, rows_all, 2 * width),
        token_grad[:, None],
    )


def solution(mesh):
    in_specs = (
        P(("rep", "exp"), None),
        P(("rep", "exp"), None),
        P(("rep", "exp"), None),
        P("exp", None, None),
        P("rep", "exp", None, None),
    )
    out_specs = (P("exp", "rep", None), P("rep", "exp", None, None), P(("rep", "exp"), None))
    return jax.shard_map(shards, mesh=mesh, in_specs=in_specs, out_specs=out_specs, check_vma=False)
```

```python
import jax
import jax.numpy as jnp
from jax import lax
from jax.experimental import pallas as pl
from jax.experimental.pallas import tpu as pltpu
from jax.sharding import PartitionSpec as P

WHOLE_VMEM = pl.BlockSpec(memory_space=pltpu.VMEM)
IN_PLACE = pl.BlockSpec(memory_space=pl.ANY)
SMALL = pl.CostEstimate(flops=1024, bytes_accessed=1024, transcendentals=0)
LARGE = pl.CostEstimate(flops=10**10, bytes_accessed=1024, transcendentals=0)


def swap(value, axis, step):
    n = lax.axis_size(axis)
    return lax.ppermute(value, axis, [(i, i ^ step) for i in range(n)])


def kernel_call(kernel, outs, operands, name, cost=SMALL, vmem=24, **more):
    more.setdefault("in_specs", [WHOLE_VMEM] * len(operands))
    more.setdefault("out_specs", [WHOLE_VMEM] * len(outs))
    return pl.pallas_call(
        kernel,
        out_shape=outs,
        compiler_params=pltpu.CompilerParams(vmem_limit_bytes=vmem * 1024 * 1024),
        cost_estimate=cost,
        name=name,
        **more,
    )(*operands)


def copy_kernel(rows, out):
    out[...] = rows[...]


def hidden_kernel(saved, hidden):
    for k in range(saved.shape[0]):
        gate, up, sigmoid = gate_parts(saved[k])
        hidden[k] = (gate * sigmoid * up).astype(jnp.bfloat16)


def place_kernel(cap, order, cot, cot_sib, routes, routes_sib, weights, weights_sib, *outs):
    chips = len(order)
    blocks, slots_out, last_out = outs[:chips], outs[chips], outs[chips + 1]
    me, mine = lax.axis_index("exp"), lax.axis_index("rep")
    chip, core = me // 2, lax.rem(me, 2)
    replicas, pair, share = blocks[0].shape
    tokens = cot.shape[0]
    before = (
        lax.broadcasted_iota(jnp.int32, (tokens, tokens), 0)
        < lax.broadcasted_iota(jnp.int32, (tokens, tokens), 1)
    ).astype(jnp.bfloat16)
    placements = []
    for i, (ids, gains) in enumerate(((routes, weights), (routes_sib, weights_sib))):
        expert = ids[...]
        weight = gains[...].astype(jnp.bfloat16).astype(jnp.float32)
        hot = lax.broadcasted_iota(jnp.int32, (2 * chips, tokens), 0) == expert
        earlier = jnp.dot(hot.astype(jnp.bfloat16), before, preferred_element_type=jnp.float32)
        position = jnp.sum(jnp.where(hot, earlier, 0.0), axis=0, keepdims=True).astype(jnp.int32)
        source = core if i == 0 else 1 - core
        step = (expert >> 1) ^ chip
        same = (expert & 1) == core
        rank = sum(jnp.where(step == k, i, 0) for i, k in enumerate(order))
        slot = jnp.where(same, rank * pair + source * cap + position, -1)
        slots_out[i : i + 1, :] = slot
        if i == 0:
            last_out[...] = jnp.where(
                step == order[-1], jnp.where(same, position, cap + position), -1
            )
        here = lax.broadcasted_iota(jnp.int32, (chips * pair, tokens), 0) == slot
        placements.append(jnp.where(here, weight, 0.0).astype(jnp.bfloat16))
    placement = jnp.concatenate(placements, axis=1)
    for j in range(replicas):
        columns = pl.ds(pl.multiple_of((mine ^ j) * share, share), share)
        rows = jnp.concatenate([cot[:, columns], cot_sib[:, columns]], axis=0)
        sent = jnp.dot(placement, rows, preferred_element_type=jnp.float32).astype(jnp.bfloat16)
        for k in range(chips):
            blocks[k][j] = sent[k * pair : (k + 1) * pair]


def products(arrived, down):
    mine = lax.axis_index("rep")
    replicas, _, share = arrived[0].shape
    pulled = 0
    for j in range(replicas):
        rows = jnp.concatenate([ref[j] for ref in arrived], axis=0)
        begin = pl.multiple_of((mine ^ j) * share, share)
        pulled += jnp.dot(rows, down[0, pl.ds(begin, share), :], preferred_element_type=jnp.float32)
    return pulled


def gate_parts(saved):
    width = saved.shape[1] // 2
    gate, up = saved[:, :width].astype(jnp.float32), saved[:, width:].astype(jnp.float32)
    sigmoid = 1.0 / (1.0 + jnp.exp(-gate))
    return gate, up, sigmoid


def router_sums(pulled, saved):
    gate, up, sigmoid = gate_parts(saved)
    return lax.dot_general(
        jnp.ones((8, pulled.shape[1]), jnp.float32),
        pulled * (gate * sigmoid * up),
        (((1,), (1,)), ((), ())),
        precision=lax.Precision.HIGHEST,
        preferred_element_type=jnp.float32,
    )[0:1]


def pair_grads(pulled, saved):
    gate, up, sigmoid = gate_parts(saved)
    both = [pulled * up * sigmoid * (1.0 + gate * (1.0 - sigmoid)), pulled * (gate * sigmoid)]
    return jnp.concatenate(both, axis=1).astype(jnp.bfloat16)


def pull_early_kernel(steps, *refs):
    count = len(steps)
    arrived, (down, saved, grads), routers = refs[:count], refs[count : count + 3], refs[count + 3 :]
    chip = lax.axis_index("exp") // 2
    pulled = products(arrived, down)
    pair = arrived[0].shape[1]
    for i, k in enumerate(steps):
        part = pulled[i * pair : (i + 1) * pair]
        routers[i][...] = router_sums(part, saved[chip ^ k])
        grads[chip ^ k] = pair_grads(part, saved[chip ^ k])


def pull_last_kernel(step, arrived, down, saved, pulled, same, other):
    me = lax.axis_index("exp")
    chip, core = me // 2, lax.rem(me, 2)
    pulled[...] = products([arrived], down)
    router = router_sums(pulled[...], saved[chip ^ step])
    cap = router.shape[1] // 2
    same[...] = jnp.where(core == 0, router[:, :cap], router[:, cap:])
    other[...] = jnp.where(core == 0, router[:, cap:], router[:, :cap])


def stack_kernel(count, *refs):
    for j, out in enumerate(refs[count:]):
        out[...] = jnp.concatenate([ref[j] for ref in refs[:count]], axis=0)


def stack(rows):
    replicas, pair, share = rows[0].shape
    return kernel_call(
        lambda *refs: stack_kernel(len(rows), *refs),
        [jax.ShapeDtypeStruct((len(rows) * pair, share), jnp.bfloat16)] * replicas,
        rows,
        "stack",
    )


def units_kernel(order, *refs):
    hidden, early, late = refs[:-2], refs[-2], refs[-1]
    chip = lax.axis_index("exp") // 2
    early[...] = jnp.concatenate([ref[chip ^ k] for ref in hidden for k in order[:-1]], axis=0)
    late[...] = jnp.concatenate([ref[chip ^ order[-1]] for ref in hidden], axis=0)


def weight_early_kernel(*refs):
    rows, units, out = refs[:-2], refs[-2], refs[-1]
    out[...] = lax.dot_general(
        jnp.concatenate([ref[...] for ref in rows], axis=0),
        units[...],
        (((0,), (0,)), ((), ())),
        preferred_element_type=jnp.float32,
    )


def finish_kernel(step, replicas, parts, *refs):
    rows = refs[:replicas][::-1]
    units, early, pulled, saved, _, out, grads, held, held_grads, sems = refs[replicas:]
    size = early.shape[0] // parts
    copies = []
    for i in range(parts):
        span = pl.ds(i * size, size)
        left = jnp.concatenate([ref[:, i * size : (i + 1) * size] for ref in rows], axis=0)
        held[span, :] = early[span, :] + lax.dot_general(
            left, units[...], (((0,), (0,)), ((), ())), preferred_element_type=jnp.float32
        )
        copies.append(pltpu.make_async_copy(held.at[span, :], out.at[0, span, :], sems.at[i]))
        copies[-1].start()
        if i == 0:
            place = (lax.axis_index("exp") // 2) ^ step
            held_grads[...] = pair_grads(pulled[...], saved[place])
            copies.append(pltpu.make_async_copy(held_grads, grads.at[place], sems.at[parts]))
            copies[-1].start()
    for copy in copies:
        copy.wait()


def token_kernel(same, other, last_slots, own, sib, weights, out):
    values = jnp.concatenate([same[...], other[...]], axis=1)
    hot = lax.broadcasted_iota(jnp.int32, (values.shape[1], out.shape[1]), 0) == last_slots[...]
    found = lax.dot_general(
        jnp.broadcast_to(values, (8, values.shape[1])),
        hot.astype(jnp.float32),
        (((1,), (0,)), ((), ())),
        precision=lax.Precision.HIGHEST,
        preferred_element_type=jnp.float32,
    )[0:1]
    weight = weights[...].astype(jnp.bfloat16).astype(jnp.float32)
    out[...] = (own[...] + sib[...] + found) / weight


def shards(cotangent, routes, gate_weight, down_weight, saved_pre):
    peers = lax.axis_size("exp")
    replicas = lax.axis_size("rep")
    rows_all = saved_pre.shape[2]
    cap = rows_all // peers
    chips = peers // 2
    pair = 2 * cap
    if pair % 16:
        return plain_shards(cotangent, routes, gate_weight, down_weight, saved_pre)
    width = down_weight.shape[2]
    tokens, model = cotangent.shape
    share = model // replicas

    last = chips // 2
    early = [k for k in range(chips) if k != last]
    order = early + [last]

    routes = routes.reshape(1, tokens)
    weights = gate_weight.reshape(1, tokens)
    cot_sib = swap(cotangent, "exp", 1)
    routes_sib = swap(routes, "exp", 1)
    weights_sib = swap(weights, "exp", 1)
    own_rows = kernel_call(
        copy_kernel,
        [jax.ShapeDtypeStruct((tokens, model), jnp.bfloat16)],
        [cotangent],
        "own_rows",
        LARGE,
    )[0]
    *blocks, slots, last_slots = kernel_call(
        lambda *refs: place_kernel(cap, order, *refs),
        [jax.ShapeDtypeStruct((replicas, pair, share), jnp.bfloat16)] * chips
        + [
            jax.ShapeDtypeStruct((2, tokens), jnp.int32),
            jax.ShapeDtypeStruct((1, tokens), jnp.int32),
        ],
        [own_rows, cot_sib, routes, routes_sib, weights, weights_sib],
        "place",
    )

    blocks = dict(zip(order, blocks))
    arrived = {0: blocks[0]}
    for k in reversed(early[1:]):
        arrived[k] = swap(blocks[k], "exp", 2 * k)
    saved = saved_pre.reshape(chips, pair, 2 * width)
    saved, slots = lax.optimization_barrier((saved, slots))
    hidden = kernel_call(
        hidden_kernel,
        [jax.ShapeDtypeStruct((chips, pair, width), jnp.bfloat16)],
        [saved],
        "hidden",
    )[0]
    hidden_of = [hidden] + [swap(hidden, "rep", j) for j in range(1, replicas)]
    units, units_last = kernel_call(
        lambda *refs: units_kernel(order, *refs),
        [
            jax.ShapeDtypeStruct((replicas * len(early) * pair, width), jnp.bfloat16),
            jax.ShapeDtypeStruct((replicas * pair, width), jnp.bfloat16),
        ],
        hidden_of,
        "units",
    )

    rows, last_block, units = lax.optimization_barrier(
        ([arrived[k] for k in early], blocks[last], units)
    )
    arrived = dict(zip(early, rows))
    last_rows = swap(last_block, "exp", 2 * last)
    early_rows = stack(rows)
    early_rows = [early_rows[0]] + [swap(early_rows[j], "rep", j) for j in range(1, replicas)]
    grads, *routers = kernel_call(
        lambda *refs: pull_early_kernel(early, *refs),
        [jax.ShapeDtypeStruct(saved.shape, jnp.bfloat16)]
        + [jax.ShapeDtypeStruct((1, pair), jnp.float32)] * len(early),
        [*[arrived[k] for k in early], down_weight, saved],
        "pull_early",
    )
    returned = routers[:1] + [swap(router, "exp", 2 * k) for router, k in zip(routers[1:], early[1:])]
    total = kernel_call(
        weight_early_kernel,
        [jax.ShapeDtypeStruct((share, width), jnp.float32)],
        [*early_rows, units],
        "weight_early",
    )[0]

    rows, grads, total, returned = lax.optimization_barrier(
        (last_rows, grads, total, returned[::-1])
    )
    returned = returned[::-1]
    late_rows = [rows[0]] + [swap(rows[j], "rep", j) for j in range(1, replicas)]
    pulled, *routers = kernel_call(
        lambda *refs: pull_last_kernel(last, *refs),
        [jax.ShapeDtypeStruct((pair, width), jnp.float32)]
        + [jax.ShapeDtypeStruct((1, cap), jnp.float32)] * 2,
        [rows, down_weight, saved],
        "pull_last",
    )
    returned = jnp.concatenate(returned, axis=1).reshape(len(early) * pair, 1)
    slot_index = lax.broadcasted_iota(jnp.int32, (len(early) * pair, 1), 0)
    sums = [
        jnp.sum(jnp.where(slot_index == ids, returned, 0.0), axis=0, keepdims=True)
        for ids in (slots[0:1], slots[1:2])
    ]
    sum_sib = swap(sums[1], "exp", 1)
    routers, sum_sib = lax.optimization_barrier((routers, sum_sib))
    returned_last = [swap(routers[i], "exp", 2 * last + i) for i in range(2)]
    parts = 4
    weight_grad, grads = kernel_call(
        lambda *refs: finish_kernel(last, replicas, parts, *refs),
        [
            jax.ShapeDtypeStruct((1, share, width), jnp.float32),
            jax.ShapeDtypeStruct(saved.shape, jnp.bfloat16),
        ],
        [*reversed(late_rows), units_last, total, pulled, saved, grads],
        "finish",
        LARGE,
        in_specs=[WHOLE_VMEM] * (replicas + 4) + [IN_PLACE],
        out_specs=[IN_PLACE] * 2,
        input_output_aliases={replicas + 4: 1},
        scratch_shapes=[
            pltpu.VMEM((share, width), jnp.float32),
            pltpu.VMEM((pair, 2 * width), jnp.bfloat16),
            pltpu.SemaphoreType.DMA((parts + 1,)),
        ],
    )
    returned_last, weight_grad = lax.optimization_barrier((returned_last, weight_grad))
    token_grad = kernel_call(
        token_kernel,
        [jax.ShapeDtypeStruct((1, tokens), jnp.float32)],
        [*returned_last, last_slots, sums[0], sum_sib, weights],
        "token",
    )[0]
    return (weight_grad, grads.reshape(1, 1, rows_all, 2 * width), token_grad.reshape(tokens, 1))


def plain_shards(cotangent, routes, gate_weight, down_weight, saved_pre):
    peers = lax.axis_size("exp")
    replicas = lax.axis_size("rep")
    me = lax.axis_index("exp")
    mine = lax.axis_index("rep")
    rows_all = saved_pre.shape[2]
    capacity = rows_all // peers
    width = down_weight.shape[2]
    model = cotangent.shape[1]
    share = model // replicas

    expert_ids = routes[:, 0]
    experts = lax.broadcasted_iota(jnp.int32, (1, peers), 1)
    one_hot = (expert_ids[:, None] == experts).astype(jnp.int32)
    earlier = jnp.cumsum(one_hot, axis=0) - one_hot
    position = jnp.sum(earlier * one_hot, axis=1)
    slot_ids = (expert_ids ^ me) * capacity + position
    slot_index = lax.broadcasted_iota(jnp.int32, (rows_all, 1), 0)
    placement = slot_index == slot_ids[None, :]
    weight = gate_weight[:, 0].astype(jnp.bfloat16)
    outgoing = jnp.dot(
        jnp.where(placement, weight[None, :], 0), cotangent, preferred_element_type=jnp.float32
    ).astype(jnp.bfloat16)
    outgoing = outgoing.reshape(peers, capacity, model)

    groups = [
        list(range(0, peers // 2)),
        list(range(peers // 2, peers // 4 * 3)),
        list(range(peers // 4 * 3, peers)),
    ]
    arrived = {0: outgoing[0]}
    for k in groups[1] + groups[2] + groups[0][1:]:
        arrived[k] = swap(outgoing[k], "exp", k)

    saved = saved_pre[0, 0].reshape(peers, capacity, 2 * width)
    saved = jnp.take(saved, jnp.arange(peers) ^ me, axis=0).reshape(rows_all, 2 * width)
    saved = saved.astype(jnp.float32)
    gate_pre = saved[:, :width]
    up_pre = saved[:, width:]
    sigmoid_gate = jax.nn.sigmoid(gate_pre)
    silu_gate = gate_pre * sigmoid_gate
    hidden = silu_gate * up_pre
    hidden_sent = hidden.astype(jnp.bfloat16)
    hidden_of = [hidden_sent] + [swap(hidden_sent, "rep", j) for j in range(1, replicas)]
    gate_factor = up_pre * sigmoid_gate * (1.0 + gate_pre * (1.0 - sigmoid_gate))

    total = 0
    pulled_parts = []
    returned = []
    for group in groups:
        begin, end = group[0] * capacity, (group[-1] + 1) * capacity
        rows = jnp.concatenate([arrived[k] for k in group], axis=0)
        columns = [
            lax.dynamic_slice_in_dim(rows, (mine ^ j) * share, share, 1) for j in range(replicas)
        ]
        left = [columns[0]] + [swap(columns[j], "rep", j) for j in range(1, replicas)]
        right = [hidden_of[j][begin:end] for j in range(replicas)]
        total = total + lax.dot_general(
            jnp.concatenate(left, axis=0),
            jnp.concatenate(right, axis=0),
            (((0,), (0,)), ((), ())),
            preferred_element_type=jnp.float32,
        )
        pulled = jnp.dot(rows, down_weight[0], preferred_element_type=jnp.float32)
        pulled_parts.append(pulled)
        router = jnp.sum(pulled * hidden[begin:end], axis=1).reshape(len(group), capacity)
        returned += [router[i] if k == 0 else swap(router[i], "exp", k) for i, k in enumerate(group)]
    pulled = jnp.concatenate(pulled_parts, axis=0)
    pair_grads = jnp.concatenate([pulled * gate_factor, pulled * silu_gate], axis=1).astype(
        jnp.bfloat16
    )
    pair_grads = pair_grads.reshape(peers, capacity, 2 * width)
    pair_grads = jnp.take(pair_grads, jnp.arange(peers) ^ me, axis=0)
    returned_grad = jnp.concatenate(returned, axis=0)
    token_grad = jnp.sum(jnp.where(placement, returned_grad[:, None], 0.0), axis=0)
    token_grad = token_grad / weight.astype(jnp.float32)
    return (
        total[None],
        pair_grads.reshape(1, 1, rows_all, 2 * width),
        token_grad[:, None],
    )


def solution(mesh):
    in_specs = (
        P(("rep", "exp"), None),
        P(("rep", "exp"), None),
        P(("rep", "exp"), None),
        P("exp", None, None),
        P("rep", "exp", None, None),
    )
    out_specs = (P("exp", "rep", None), P("rep", "exp", None, None), P(("rep", "exp"), None))
    return jax.shard_map(shards, mesh=mesh, in_specs=in_specs, out_specs=out_specs, check_vma=False)
```

```python
import jax
import jax.numpy as jnp
from jax import lax
from jax.experimental import pallas as pl
from jax.experimental.pallas import tpu as pltpu
from jax.sharding import PartitionSpec as P

WHOLE_VMEM = pl.BlockSpec(memory_space=pltpu.VMEM)
IN_PLACE = pl.BlockSpec(memory_space=pl.ANY)
SMALL = pl.CostEstimate(flops=1024, bytes_accessed=1024, transcendentals=0)
LARGE = pl.CostEstimate(flops=10**10, bytes_accessed=1024, transcendentals=0)


def swap(value, axis, step):
    n = lax.axis_size(axis)
    return lax.ppermute(value, axis, [(i, i ^ step) for i in range(n)])


def kernel_call(kernel, outs, operands, name, cost=SMALL, vmem=24, **more):
    more.setdefault("in_specs", [WHOLE_VMEM] * len(operands))
    more.setdefault("out_specs", [WHOLE_VMEM] * len(outs))
    return pl.pallas_call(
        kernel,
        out_shape=outs,
        compiler_params=pltpu.CompilerParams(vmem_limit_bytes=vmem * 1024 * 1024),
        cost_estimate=cost,
        name=name,
        **more,
    )(*operands)


def copy_kernel(rows, out):
    out[...] = rows[...]


def hidden_kernel(saved, hidden):
    for k in range(saved.shape[0]):
        gate, up, sigmoid = gate_parts(saved[k])
        hidden[k] = (gate * sigmoid * up).astype(jnp.bfloat16)


def place_kernel(cap, order, cot, cot_sib, routes, routes_sib, weights, weights_sib, *outs):
    chips = len(order)
    blocks, slots_out, last_out = outs[:chips], outs[chips], outs[chips + 1]
    me, mine = lax.axis_index("exp"), lax.axis_index("rep")
    chip, core = me // 2, lax.rem(me, 2)
    replicas, pair, share = blocks[0].shape
    tokens = cot.shape[0]
    before = (
        lax.broadcasted_iota(jnp.int32, (tokens, tokens), 0)
        < lax.broadcasted_iota(jnp.int32, (tokens, tokens), 1)
    ).astype(jnp.bfloat16)
    placements = []
    for i, (ids, gains) in enumerate(((routes, weights), (routes_sib, weights_sib))):
        expert = ids[...]
        weight = gains[...].astype(jnp.bfloat16).astype(jnp.float32)
        hot = lax.broadcasted_iota(jnp.int32, (2 * chips, tokens), 0) == expert
        earlier = jnp.dot(hot.astype(jnp.bfloat16), before, preferred_element_type=jnp.float32)
        position = jnp.sum(jnp.where(hot, earlier, 0.0), axis=0, keepdims=True).astype(jnp.int32)
        source = core if i == 0 else 1 - core
        step = (expert >> 1) ^ chip
        same = (expert & 1) == core
        rank = sum(jnp.where(step == k, i, 0) for i, k in enumerate(order))
        slot = jnp.where(same, rank * pair + source * cap + position, -1)
        slots_out[i : i + 1, :] = slot
        if i == 0:
            last_out[...] = jnp.where(
                step == order[-1], jnp.where(same, position, cap + position), -1
            )
        here = lax.broadcasted_iota(jnp.int32, (chips * pair, tokens), 0) == slot
        placements.append(jnp.where(here, weight, 0.0).astype(jnp.bfloat16))
    placement = jnp.concatenate(placements, axis=1)
    for j in range(replicas):
        columns = pl.ds(pl.multiple_of((mine ^ j) * share, share), share)
        rows = jnp.concatenate([cot[:, columns], cot_sib[:, columns]], axis=0)
        sent = jnp.dot(placement, rows, preferred_element_type=jnp.float32).astype(jnp.bfloat16)
        for k in range(chips):
            blocks[k][j] = sent[k * pair : (k + 1) * pair]


def products(arrived, down):
    mine = lax.axis_index("rep")
    replicas, _, share = arrived[0].shape
    pulled = 0
    for j in range(replicas):
        rows = jnp.concatenate([ref[j] for ref in arrived], axis=0)
        begin = pl.multiple_of((mine ^ j) * share, share)
        pulled += jnp.dot(rows, down[0, pl.ds(begin, share), :], preferred_element_type=jnp.float32)
    return pulled


def gate_parts(saved):
    width = saved.shape[1] // 2
    gate, up = saved[:, :width].astype(jnp.float32), saved[:, width:].astype(jnp.float32)
    sigmoid = 1.0 / (1.0 + jnp.exp(-gate))
    return gate, up, sigmoid


def router_sums(pulled, saved):
    gate, up, sigmoid = gate_parts(saved)
    return lax.dot_general(
        jnp.ones((8, pulled.shape[1]), jnp.float32),
        pulled * (gate * sigmoid * up),
        (((1,), (1,)), ((), ())),
        precision=lax.Precision.HIGHEST,
        preferred_element_type=jnp.float32,
    )[0:1]


def pair_grads(pulled, saved):
    gate, up, sigmoid = gate_parts(saved)
    both = [pulled * up * sigmoid * (1.0 + gate * (1.0 - sigmoid)), pulled * (gate * sigmoid)]
    return jnp.concatenate(both, axis=1).astype(jnp.bfloat16)


def pull_early_kernel(steps, *refs):
    count = len(steps)
    arrived, (down, saved, grads), routers = refs[:count], refs[count : count + 3], refs[count + 3 :]
    chip = lax.axis_index("exp") // 2
    pulled = products(arrived, down)
    pair = arrived[0].shape[1]
    for i, k in enumerate(steps):
        part = pulled[i * pair : (i + 1) * pair]
        routers[i][...] = router_sums(part, saved[chip ^ k])
        grads[chip ^ k] = pair_grads(part, saved[chip ^ k])


def pull_last_kernel(step, arrived, down, saved, pulled, same, other):
    me = lax.axis_index("exp")
    chip, core = me // 2, lax.rem(me, 2)
    pulled[...] = products([arrived], down)
    router = router_sums(pulled[...], saved[chip ^ step])
    cap = router.shape[1] // 2
    same[...] = jnp.where(core == 0, router[:, :cap], router[:, cap:])
    other[...] = jnp.where(core == 0, router[:, cap:], router[:, :cap])


def stack_kernel(count, *refs):
    for j, out in enumerate(refs[count:]):
        out[...] = jnp.concatenate([ref[j] for ref in refs[:count]], axis=0)


def stack(rows):
    replicas, pair, share = rows[0].shape
    return kernel_call(
        lambda *refs: stack_kernel(len(rows), *refs),
        [jax.ShapeDtypeStruct((len(rows) * pair, share), jnp.bfloat16)] * replicas,
        rows,
        "stack",
    )


def units_kernel(order, *refs):
    hidden, early, late = refs[-3::-1], refs[-2], refs[-1]
    chip = lax.axis_index("exp") // 2
    early[...] = jnp.concatenate([ref[chip ^ k] for ref in hidden for k in order[:-1]], axis=0)
    late[...] = jnp.concatenate([ref[chip ^ order[-1]] for ref in hidden], axis=0)


def weight_early_kernel(*refs):
    rows, units, out = refs[:-2], refs[-2], refs[-1]
    out[...] = lax.dot_general(
        jnp.concatenate([ref[...] for ref in rows], axis=0),
        units[...],
        (((0,), (0,)), ((), ())),
        preferred_element_type=jnp.float32,
    )


def finish_kernel(step, replicas, parts, *refs):
    rows = refs[:replicas][::-1]
    units, early, pulled, saved, _, out, grads, held, held_grads, sems = refs[replicas:]
    size = early.shape[0] // parts
    copies = []
    for i in range(parts):
        span = pl.ds(i * size, size)
        left = jnp.concatenate([ref[:, i * size : (i + 1) * size] for ref in rows], axis=0)
        held[span, :] = early[span, :] + lax.dot_general(
            left, units[...], (((0,), (0,)), ((), ())), preferred_element_type=jnp.float32
        )
        copies.append(pltpu.make_async_copy(held.at[span, :], out.at[0, span, :], sems.at[i]))
        copies[-1].start()
        if i == 0:
            place = (lax.axis_index("exp") // 2) ^ step
            held_grads[...] = pair_grads(pulled[...], saved[place])
            copies.append(pltpu.make_async_copy(held_grads, grads.at[place], sems.at[parts]))
            copies[-1].start()
    for copy in copies:
        copy.wait()


def token_kernel(same, other, last_slots, own, sib, weights, out):
    values = jnp.concatenate([same[...], other[...]], axis=1)
    hot = lax.broadcasted_iota(jnp.int32, (values.shape[1], out.shape[1]), 0) == last_slots[...]
    found = lax.dot_general(
        jnp.broadcast_to(values, (8, values.shape[1])),
        hot.astype(jnp.float32),
        (((1,), (0,)), ((), ())),
        precision=lax.Precision.HIGHEST,
        preferred_element_type=jnp.float32,
    )[0:1]
    weight = weights[...].astype(jnp.bfloat16).astype(jnp.float32)
    out[...] = (own[...] + sib[...] + found) / weight


def shards(cotangent, routes, gate_weight, down_weight, saved_pre):
    peers = lax.axis_size("exp")
    replicas = lax.axis_size("rep")
    rows_all = saved_pre.shape[2]
    cap = rows_all // peers
    chips = peers // 2
    pair = 2 * cap
    if pair % 16:
        return plain_shards(cotangent, routes, gate_weight, down_weight, saved_pre)
    width = down_weight.shape[2]
    tokens, model = cotangent.shape
    share = model // replicas

    last = chips // 2
    early = [k for k in range(chips) if k != last]
    order = early + [last]

    routes = routes.reshape(1, tokens)
    weights = gate_weight.reshape(1, tokens)
    cot_sib = swap(cotangent, "exp", 1)
    routes_sib = swap(routes, "exp", 1)
    weights_sib = swap(weights, "exp", 1)
    own_rows = kernel_call(
        copy_kernel,
        [jax.ShapeDtypeStruct((tokens, model), jnp.bfloat16)],
        [cotangent],
        "own_rows",
        LARGE,
    )[0]
    *blocks, slots, last_slots = kernel_call(
        lambda *refs: place_kernel(cap, order, *refs),
        [jax.ShapeDtypeStruct((replicas, pair, share), jnp.bfloat16)] * chips
        + [
            jax.ShapeDtypeStruct((2, tokens), jnp.int32),
            jax.ShapeDtypeStruct((1, tokens), jnp.int32),
        ],
        [own_rows, cot_sib, routes, routes_sib, weights, weights_sib],
        "place",
    )

    blocks = dict(zip(order, blocks))
    arrived = {0: blocks[0]}
    for k in reversed(early[1:]):
        arrived[k] = swap(blocks[k], "exp", 2 * k)
    saved = saved_pre.reshape(chips, pair, 2 * width)
    saved, slots = lax.optimization_barrier((saved, slots))
    hidden = kernel_call(
        hidden_kernel,
        [jax.ShapeDtypeStruct((chips, pair, width), jnp.bfloat16)],
        [saved],
        "hidden",
    )[0]
    hidden_of = [hidden] + [swap(hidden, "rep", j) for j in range(1, replicas)]
    units, units_last = kernel_call(
        lambda *refs: units_kernel(order, *refs),
        [
            jax.ShapeDtypeStruct((replicas * len(early) * pair, width), jnp.bfloat16),
            jax.ShapeDtypeStruct((replicas * pair, width), jnp.bfloat16),
        ],
        hidden_of[::-1],
        "units",
    )

    rows, last_block, units = lax.optimization_barrier(
        ([arrived[k] for k in early], blocks[last], units)
    )
    arrived = dict(zip(early, rows))
    last_rows = swap(last_block, "exp", 2 * last)
    early_rows = stack(rows)
    early_rows = [early_rows[0]] + [swap(early_rows[j], "rep", j) for j in range(1, replicas)]
    grads, *routers = kernel_call(
        lambda *refs: pull_early_kernel(early, *refs),
        [jax.ShapeDtypeStruct(saved.shape, jnp.bfloat16)]
        + [jax.ShapeDtypeStruct((1, pair), jnp.float32)] * len(early),
        [*[arrived[k] for k in early], down_weight, saved],
        "pull_early",
    )
    returned = routers[:1] + [swap(router, "exp", 2 * k) for router, k in zip(routers[1:], early[1:])]
    total = kernel_call(
        weight_early_kernel,
        [jax.ShapeDtypeStruct((share, width), jnp.float32)],
        [*early_rows, units],
        "weight_early",
    )[0]

    rows, grads, total, near_returned = lax.optimization_barrier(
        (last_rows, grads, total, returned[:2])
    )
    returned = [*near_returned, *returned[2:]]
    late_rows = [rows[0]] + [swap(rows[j], "rep", j) for j in range(1, replicas)]
    returned = jnp.concatenate(returned, axis=1).reshape(len(early) * pair, 1)
    slot_index = lax.broadcasted_iota(jnp.int32, (len(early) * pair, 1), 0)
    sums = [
        jnp.sum(jnp.where(slot_index == ids, returned, 0.0), axis=0, keepdims=True)
        for ids in (slots[0:1], slots[1:2])
    ]
    rows, sums = lax.optimization_barrier((rows, sums))
    pulled, *routers = kernel_call(
        lambda *refs: pull_last_kernel(last, *refs),
        [jax.ShapeDtypeStruct((pair, width), jnp.float32)]
        + [jax.ShapeDtypeStruct((1, cap), jnp.float32)] * 2,
        [rows, down_weight, saved],
        "pull_last",
    )
    returned_last = [swap(routers[i], "exp", 2 * last + i) for i in range(2)]
    late_rows, sum_sib = lax.optimization_barrier((late_rows[::-1], sums[1]))
    late_rows = late_rows[::-1]
    sum_sib = swap(sum_sib, "exp", 1)
    parts = 4
    weight_grad, grads = kernel_call(
        lambda *refs: finish_kernel(last, replicas, parts, *refs),
        [
            jax.ShapeDtypeStruct((1, share, width), jnp.float32),
            jax.ShapeDtypeStruct(saved.shape, jnp.bfloat16),
        ],
        [*reversed(late_rows), units_last, total, pulled, saved, grads],
        "finish",
        LARGE,
        in_specs=[WHOLE_VMEM] * (replicas + 4) + [IN_PLACE],
        out_specs=[IN_PLACE] * 2,
        input_output_aliases={replicas + 4: 1},
        scratch_shapes=[
            pltpu.VMEM((share, width), jnp.float32),
            pltpu.VMEM((pair, 2 * width), jnp.bfloat16),
            pltpu.SemaphoreType.DMA((parts + 1,)),
        ],
    )
    returned_last, weight_grad = lax.optimization_barrier((returned_last, weight_grad))
    token_grad = kernel_call(
        token_kernel,
        [jax.ShapeDtypeStruct((1, tokens), jnp.float32)],
        [*returned_last, last_slots, sums[0], sum_sib, weights],
        "token",
    )[0]
    return (weight_grad, grads.reshape(1, 1, rows_all, 2 * width), token_grad.reshape(tokens, 1))


def plain_shards(cotangent, routes, gate_weight, down_weight, saved_pre):
    peers = lax.axis_size("exp")
    replicas = lax.axis_size("rep")
    me = lax.axis_index("exp")
    mine = lax.axis_index("rep")
    rows_all = saved_pre.shape[2]
    capacity = rows_all // peers
    width = down_weight.shape[2]
    model = cotangent.shape[1]
    share = model // replicas

    expert_ids = routes[:, 0]
    experts = lax.broadcasted_iota(jnp.int32, (1, peers), 1)
    one_hot = (expert_ids[:, None] == experts).astype(jnp.int32)
    earlier = jnp.cumsum(one_hot, axis=0) - one_hot
    position = jnp.sum(earlier * one_hot, axis=1)
    slot_ids = (expert_ids ^ me) * capacity + position
    slot_index = lax.broadcasted_iota(jnp.int32, (rows_all, 1), 0)
    placement = slot_index == slot_ids[None, :]
    weight = gate_weight[:, 0].astype(jnp.bfloat16)
    outgoing = jnp.dot(
        jnp.where(placement, weight[None, :], 0), cotangent, preferred_element_type=jnp.float32
    ).astype(jnp.bfloat16)
    outgoing = outgoing.reshape(peers, capacity, model)

    groups = [
        list(range(0, peers // 2)),
        list(range(peers // 2, peers // 4 * 3)),
        list(range(peers // 4 * 3, peers)),
    ]
    arrived = {0: outgoing[0]}
    for k in groups[1] + groups[2] + groups[0][1:]:
        arrived[k] = swap(outgoing[k], "exp", k)

    saved = saved_pre[0, 0].reshape(peers, capacity, 2 * width)
    saved = jnp.take(saved, jnp.arange(peers) ^ me, axis=0).reshape(rows_all, 2 * width)
    saved = saved.astype(jnp.float32)
    gate_pre = saved[:, :width]
    up_pre = saved[:, width:]
    sigmoid_gate = jax.nn.sigmoid(gate_pre)
    silu_gate = gate_pre * sigmoid_gate
    hidden = silu_gate * up_pre
    hidden_sent = hidden.astype(jnp.bfloat16)
    hidden_of = [hidden_sent] + [swap(hidden_sent, "rep", j) for j in range(1, replicas)]
    gate_factor = up_pre * sigmoid_gate * (1.0 + gate_pre * (1.0 - sigmoid_gate))

    total = 0
    pulled_parts = []
    returned = []
    for group in groups:
        begin, end = group[0] * capacity, (group[-1] + 1) * capacity
        rows = jnp.concatenate([arrived[k] for k in group], axis=0)
        columns = [
            lax.dynamic_slice_in_dim(rows, (mine ^ j) * share, share, 1) for j in range(replicas)
        ]
        left = [columns[0]] + [swap(columns[j], "rep", j) for j in range(1, replicas)]
        right = [hidden_of[j][begin:end] for j in range(replicas)]
        total = total + lax.dot_general(
            jnp.concatenate(left, axis=0),
            jnp.concatenate(right, axis=0),
            (((0,), (0,)), ((), ())),
            preferred_element_type=jnp.float32,
        )
        pulled = jnp.dot(rows, down_weight[0], preferred_element_type=jnp.float32)
        pulled_parts.append(pulled)
        router = jnp.sum(pulled * hidden[begin:end], axis=1).reshape(len(group), capacity)
        returned += [router[i] if k == 0 else swap(router[i], "exp", k) for i, k in enumerate(group)]
    pulled = jnp.concatenate(pulled_parts, axis=0)
    pair_grads = jnp.concatenate([pulled * gate_factor, pulled * silu_gate], axis=1).astype(
        jnp.bfloat16
    )
    pair_grads = pair_grads.reshape(peers, capacity, 2 * width)
    pair_grads = jnp.take(pair_grads, jnp.arange(peers) ^ me, axis=0)
    returned_grad = jnp.concatenate(returned, axis=0)
    token_grad = jnp.sum(jnp.where(placement, returned_grad[:, None], 0.0), axis=0)
    token_grad = token_grad / weight.astype(jnp.float32)
    return (
        total[None],
        pair_grads.reshape(1, 1, rows_all, 2 * width),
        token_grad[:, None],
    )


def solution(mesh):
    in_specs = (
        P(("rep", "exp"), None),
        P(("rep", "exp"), None),
        P(("rep", "exp"), None),
        P("exp", None, None),
        P("rep", "exp", None, None),
    )
    out_specs = (P("exp", "rep", None), P("rep", "exp", None, None), P(("rep", "exp"), None))
    return jax.shard_map(shards, mesh=mesh, in_specs=in_specs, out_specs=out_specs, check_vma=False)
```

```python
import jax
import jax.numpy as jnp
from jax import lax
from jax.experimental import pallas as pl
from jax.experimental.pallas import tpu as pltpu
from jax.sharding import PartitionSpec as P

WHOLE_VMEM = pl.BlockSpec(memory_space=pltpu.VMEM)
IN_PLACE = pl.BlockSpec(memory_space=pl.ANY)
SMALL = pl.CostEstimate(flops=1024, bytes_accessed=1024, transcendentals=0)
LARGE = pl.CostEstimate(flops=10**10, bytes_accessed=1024, transcendentals=0)


def swap(value, axis, step):
    n = lax.axis_size(axis)
    return lax.ppermute(value, axis, [(i, i ^ step) for i in range(n)])


def kernel_call(kernel, outs, operands, name, cost=SMALL, vmem=24, **more):
    more.setdefault("in_specs", [WHOLE_VMEM] * len(operands))
    more.setdefault("out_specs", [WHOLE_VMEM] * len(outs))
    return pl.pallas_call(
        kernel,
        out_shape=outs,
        compiler_params=pltpu.CompilerParams(vmem_limit_bytes=vmem * 1024 * 1024),
        cost_estimate=cost,
        name=name,
        **more,
    )(*operands)


def copy_kernel(rows, out):
    out[...] = rows[...]


def hidden_kernel(saved, hidden):
    for k in range(saved.shape[0]):
        gate, up, sigmoid = gate_parts(saved[k])
        hidden[k] = (gate * sigmoid * up).astype(jnp.bfloat16)


def place_kernel(cap, order, cot, cot_sib, routes, routes_sib, weights, weights_sib, *outs):
    chips = len(order)
    blocks, slots_out, last_out = outs[:chips], outs[chips], outs[chips + 1]
    me, mine = lax.axis_index("exp"), lax.axis_index("rep")
    chip, core = me // 2, lax.rem(me, 2)
    replicas, pair, share = blocks[0].shape
    tokens = cot.shape[0]
    before = (
        lax.broadcasted_iota(jnp.int32, (tokens, tokens), 0)
        < lax.broadcasted_iota(jnp.int32, (tokens, tokens), 1)
    ).astype(jnp.bfloat16)
    placements = []
    for i, (ids, gains) in enumerate(((routes, weights), (routes_sib, weights_sib))):
        expert = ids[...]
        weight = gains[...].astype(jnp.bfloat16).astype(jnp.float32)
        hot = lax.broadcasted_iota(jnp.int32, (2 * chips, tokens), 0) == expert
        earlier = jnp.dot(hot.astype(jnp.bfloat16), before, preferred_element_type=jnp.float32)
        position = jnp.sum(jnp.where(hot, earlier, 0.0), axis=0, keepdims=True).astype(jnp.int32)
        source = core if i == 0 else 1 - core
        step = (expert >> 1) ^ chip
        same = (expert & 1) == core
        rank = sum(jnp.where(step == k, i, 0) for i, k in enumerate(order))
        slot = jnp.where(same, rank * pair + source * cap + position, -1)
        slots_out[i : i + 1, :] = slot
        if i == 0:
            last_out[...] = jnp.where(
                step == order[-1], jnp.where(same, position, cap + position), -1
            )
        here = lax.broadcasted_iota(jnp.int32, (chips * pair, tokens), 0) == slot
        placements.append(jnp.where(here, weight, 0.0).astype(jnp.bfloat16))
    placement = jnp.concatenate(placements, axis=1)
    for j in range(replicas):
        columns = pl.ds(pl.multiple_of((mine ^ j) * share, share), share)
        rows = jnp.concatenate([cot[:, columns], cot_sib[:, columns]], axis=0)
        sent = jnp.dot(placement, rows, preferred_element_type=jnp.float32).astype(jnp.bfloat16)
        for k in range(chips):
            blocks[k][j] = sent[k * pair : (k + 1) * pair]


def products(arrived, down):
    mine = lax.axis_index("rep")
    replicas, _, share = arrived[0].shape
    pulled = 0
    for j in range(replicas):
        rows = jnp.concatenate([ref[j] for ref in arrived], axis=0)
        begin = pl.multiple_of((mine ^ j) * share, share)
        pulled += jnp.dot(rows, down[0, pl.ds(begin, share), :], preferred_element_type=jnp.float32)
    return pulled


def gate_parts(saved):
    width = saved.shape[1] // 2
    gate, up = saved[:, :width].astype(jnp.float32), saved[:, width:].astype(jnp.float32)
    sigmoid = 1.0 / (1.0 + jnp.exp(-gate))
    return gate, up, sigmoid


def router_sums(pulled, saved):
    gate, up, sigmoid = gate_parts(saved)
    return lax.dot_general(
        jnp.ones((8, pulled.shape[1]), jnp.float32),
        pulled * (gate * sigmoid * up),
        (((1,), (1,)), ((), ())),
        precision=lax.Precision.HIGHEST,
        preferred_element_type=jnp.float32,
    )[0:1]


def pair_grads(pulled, saved):
    gate, up, sigmoid = gate_parts(saved)
    both = [pulled * up * sigmoid * (1.0 + gate * (1.0 - sigmoid)), pulled * (gate * sigmoid)]
    return jnp.concatenate(both, axis=1).astype(jnp.bfloat16)


def pull_early_kernel(steps, *refs):
    count = len(steps)
    arrived, (down, saved, grads), routers = refs[:count], refs[count : count + 3], refs[count + 3 :]
    chip = lax.axis_index("exp") // 2
    pulled = products(arrived, down)
    pair = arrived[0].shape[1]
    for i, k in enumerate(steps):
        part = pulled[i * pair : (i + 1) * pair]
        routers[i][...] = router_sums(part, saved[chip ^ k])
        grads[chip ^ k] = pair_grads(part, saved[chip ^ k])


def pull_last_kernel(step, arrived, down, saved, pulled, same, other):
    me = lax.axis_index("exp")
    chip, core = me // 2, lax.rem(me, 2)
    pulled[...] = products([arrived], down)
    router = router_sums(pulled[...], saved[chip ^ step])
    cap = router.shape[1] // 2
    same[...] = jnp.where(core == 0, router[:, :cap], router[:, cap:])
    other[...] = jnp.where(core == 0, router[:, cap:], router[:, :cap])


def stack_kernel(count, *refs):
    for j, out in enumerate(refs[count:]):
        out[...] = jnp.concatenate([ref[j] for ref in refs[:count]], axis=0)


def stack(rows):
    replicas, pair, share = rows[0].shape
    return kernel_call(
        lambda *refs: stack_kernel(len(rows), *refs),
        [jax.ShapeDtypeStruct((len(rows) * pair, share), jnp.bfloat16)] * replicas,
        rows,
        "stack",
    )


def units_kernel(order, *refs):
    hidden, early, late = refs[-3::-1], refs[-2], refs[-1]
    chip = lax.axis_index("exp") // 2
    early[...] = jnp.concatenate([ref[chip ^ k] for ref in hidden for k in order[:-1]], axis=0)
    late[...] = jnp.concatenate([ref[chip ^ order[-1]] for ref in hidden], axis=0)


def weight_early_kernel(first, rows, units, before, out):
    size = rows[0].shape[0]
    total = lax.dot_general(
        jnp.concatenate([ref[...] for ref in rows], axis=0),
        units[first * size : (first + len(rows)) * size, :],
        (((0,), (0,)), ((), ())),
        preferred_element_type=jnp.float32,
    )
    out[...] = total + before[0][...] if before else total


def finish_kernel(step, replicas, parts, *refs):
    rows = refs[:replicas][::-1]
    units, early, pulled, saved, _, out, grads, held, held_grads, sems = refs[replicas:]
    size = early.shape[0] // parts
    copies = []
    for i in range(parts):
        span = pl.ds(i * size, size)
        left = jnp.concatenate([ref[:, i * size : (i + 1) * size] for ref in rows], axis=0)
        held[span, :] = early[span, :] + lax.dot_general(
            left, units[...], (((0,), (0,)), ((), ())), preferred_element_type=jnp.float32
        )
        copies.append(pltpu.make_async_copy(held.at[span, :], out.at[0, span, :], sems.at[i]))
        copies[-1].start()
        if i == 0:
            place = (lax.axis_index("exp") // 2) ^ step
            held_grads[...] = pair_grads(pulled[...], saved[place])
            copies.append(pltpu.make_async_copy(held_grads, grads.at[place], sems.at[parts]))
            copies[-1].start()
    for copy in copies:
        copy.wait()


def token_kernel(same, other, last_slots, own, sib, weights, out):
    values = jnp.concatenate([same[...], other[...]], axis=1)
    hot = lax.broadcasted_iota(jnp.int32, (values.shape[1], out.shape[1]), 0) == last_slots[...]
    found = lax.dot_general(
        jnp.broadcast_to(values, (8, values.shape[1])),
        hot.astype(jnp.float32),
        (((1,), (0,)), ((), ())),
        precision=lax.Precision.HIGHEST,
        preferred_element_type=jnp.float32,
    )[0:1]
    weight = weights[...].astype(jnp.bfloat16).astype(jnp.float32)
    out[...] = (own[...] + sib[...] + found) / weight


def shards(cotangent, routes, gate_weight, down_weight, saved_pre):
    peers = lax.axis_size("exp")
    replicas = lax.axis_size("rep")
    rows_all = saved_pre.shape[2]
    cap = rows_all // peers
    chips = peers // 2
    pair = 2 * cap
    if pair % 16:
        return plain_shards(cotangent, routes, gate_weight, down_weight, saved_pre)
    width = down_weight.shape[2]
    tokens, model = cotangent.shape
    share = model // replicas

    last = chips // 2
    early = [k for k in range(chips) if k != last]
    order = early + [last]

    routes = routes.reshape(1, tokens)
    weights = gate_weight.reshape(1, tokens)
    cot_sib = swap(cotangent, "exp", 1)
    routes_sib = swap(routes, "exp", 1)
    weights_sib = swap(weights, "exp", 1)
    own_rows = kernel_call(
        copy_kernel,
        [jax.ShapeDtypeStruct((tokens, model), jnp.bfloat16)],
        [cotangent],
        "own_rows",
        LARGE,
    )[0]
    *blocks, slots, last_slots = kernel_call(
        lambda *refs: place_kernel(cap, order, *refs),
        [jax.ShapeDtypeStruct((replicas, pair, share), jnp.bfloat16)] * chips
        + [
            jax.ShapeDtypeStruct((2, tokens), jnp.int32),
            jax.ShapeDtypeStruct((1, tokens), jnp.int32),
        ],
        [own_rows, cot_sib, routes, routes_sib, weights, weights_sib],
        "place",
    )

    blocks = dict(zip(order, blocks))
    arrived = {0: blocks[0]}
    for k in reversed(early[1:]):
        arrived[k] = swap(blocks[k], "exp", 2 * k)
    saved = saved_pre.reshape(chips, pair, 2 * width)
    saved, slots = lax.optimization_barrier((saved, slots))
    hidden = kernel_call(
        hidden_kernel,
        [jax.ShapeDtypeStruct((chips, pair, width), jnp.bfloat16)],
        [saved],
        "hidden",
    )[0]
    hidden_of = [hidden] + [swap(hidden, "rep", j) for j in range(1, replicas)]
    units, units_last = kernel_call(
        lambda *refs: units_kernel(order, *refs),
        [
            jax.ShapeDtypeStruct((replicas * len(early) * pair, width), jnp.bfloat16),
            jax.ShapeDtypeStruct((replicas * pair, width), jnp.bfloat16),
        ],
        hidden_of[::-1],
        "units",
    )

    rows, last_block, units = lax.optimization_barrier(
        ([arrived[k] for k in early], blocks[last], units)
    )
    arrived = dict(zip(early, rows))
    last_rows = swap(last_block, "exp", 2 * last)
    early_rows = stack(rows)
    early_rows = [early_rows[0]] + [swap(early_rows[j], "rep", j) for j in range(1, replicas)]
    grads, *routers = kernel_call(
        lambda *refs: pull_early_kernel(early, *refs),
        [jax.ShapeDtypeStruct(saved.shape, jnp.bfloat16)]
        + [jax.ShapeDtypeStruct((1, pair), jnp.float32)] * len(early),
        [*[arrived[k] for k in early], down_weight, saved],
        "pull_early",
    )
    returned = routers[:1] + [swap(router, "exp", 2 * k) for router, k in zip(routers[1:], early[1:])]
    total = []
    half = replicas // 2
    for first, count in ((0, half), (half, replicas - half)):
        total = kernel_call(
            lambda *refs: weight_early_kernel(
                first, refs[:count], refs[count], refs[count + 1 : -1], refs[-1]
            ),
            [jax.ShapeDtypeStruct((share, width), jnp.float32)],
            [*early_rows[first : first + count], units, *total],
            "weight_rest" if first else "weight_first",
        )
    total = total[0]

    rows, grads, total, near_returned = lax.optimization_barrier(
        (last_rows, grads, total, returned[:2])
    )
    returned = [*near_returned, *returned[2:]]
    late_rows = [rows[0]] + [swap(rows[j], "rep", j) for j in range(1, replicas)]
    returned = jnp.concatenate(returned, axis=1).reshape(len(early) * pair, 1)
    slot_index = lax.broadcasted_iota(jnp.int32, (len(early) * pair, 1), 0)
    sums = [
        jnp.sum(jnp.where(slot_index == ids, returned, 0.0), axis=0, keepdims=True)
        for ids in (slots[0:1], slots[1:2])
    ]
    rows, sums = lax.optimization_barrier((rows, sums))
    pulled, *routers = kernel_call(
        lambda *refs: pull_last_kernel(last, *refs),
        [jax.ShapeDtypeStruct((pair, width), jnp.float32)]
        + [jax.ShapeDtypeStruct((1, cap), jnp.float32)] * 2,
        [rows, down_weight, saved],
        "pull_last",
    )
    returned_last = [swap(routers[i], "exp", 2 * last + i) for i in range(2)]
    late_rows, sum_sib = lax.optimization_barrier((late_rows[::-1], sums[1]))
    late_rows = late_rows[::-1]
    sum_sib = swap(sum_sib, "exp", 1)
    parts = 4
    weight_grad, grads = kernel_call(
        lambda *refs: finish_kernel(last, replicas, parts, *refs),
        [
            jax.ShapeDtypeStruct((1, share, width), jnp.float32),
            jax.ShapeDtypeStruct(saved.shape, jnp.bfloat16),
        ],
        [*reversed(late_rows), units_last, total, pulled, saved, grads],
        "finish",
        LARGE,
        in_specs=[WHOLE_VMEM] * (replicas + 4) + [IN_PLACE],
        out_specs=[IN_PLACE] * 2,
        input_output_aliases={replicas + 4: 1},
        scratch_shapes=[
            pltpu.VMEM((share, width), jnp.float32),
            pltpu.VMEM((pair, 2 * width), jnp.bfloat16),
            pltpu.SemaphoreType.DMA((parts + 1,)),
        ],
    )
    returned_last, weight_grad = lax.optimization_barrier((returned_last, weight_grad))
    token_grad = kernel_call(
        token_kernel,
        [jax.ShapeDtypeStruct((1, tokens), jnp.float32)],
        [*returned_last, last_slots, sums[0], sum_sib, weights],
        "token",
    )[0]
    return (weight_grad, grads.reshape(1, 1, rows_all, 2 * width), token_grad.reshape(tokens, 1))


def plain_shards(cotangent, routes, gate_weight, down_weight, saved_pre):
    peers = lax.axis_size("exp")
    replicas = lax.axis_size("rep")
    me = lax.axis_index("exp")
    mine = lax.axis_index("rep")
    rows_all = saved_pre.shape[2]
    capacity = rows_all // peers
    width = down_weight.shape[2]
    model = cotangent.shape[1]
    share = model // replicas

    expert_ids = routes[:, 0]
    experts = lax.broadcasted_iota(jnp.int32, (1, peers), 1)
    one_hot = (expert_ids[:, None] == experts).astype(jnp.int32)
    earlier = jnp.cumsum(one_hot, axis=0) - one_hot
    position = jnp.sum(earlier * one_hot, axis=1)
    slot_ids = (expert_ids ^ me) * capacity + position
    slot_index = lax.broadcasted_iota(jnp.int32, (rows_all, 1), 0)
    placement = slot_index == slot_ids[None, :]
    weight = gate_weight[:, 0].astype(jnp.bfloat16)
    outgoing = jnp.dot(
        jnp.where(placement, weight[None, :], 0), cotangent, preferred_element_type=jnp.float32
    ).astype(jnp.bfloat16)
    outgoing = outgoing.reshape(peers, capacity, model)

    groups = [
        list(range(0, peers // 2)),
        list(range(peers // 2, peers // 4 * 3)),
        list(range(peers // 4 * 3, peers)),
    ]
    arrived = {0: outgoing[0]}
    for k in groups[1] + groups[2] + groups[0][1:]:
        arrived[k] = swap(outgoing[k], "exp", k)

    saved = saved_pre[0, 0].reshape(peers, capacity, 2 * width)
    saved = jnp.take(saved, jnp.arange(peers) ^ me, axis=0).reshape(rows_all, 2 * width)
    saved = saved.astype(jnp.float32)
    gate_pre = saved[:, :width]
    up_pre = saved[:, width:]
    sigmoid_gate = jax.nn.sigmoid(gate_pre)
    silu_gate = gate_pre * sigmoid_gate
    hidden = silu_gate * up_pre
    hidden_sent = hidden.astype(jnp.bfloat16)
    hidden_of = [hidden_sent] + [swap(hidden_sent, "rep", j) for j in range(1, replicas)]
    gate_factor = up_pre * sigmoid_gate * (1.0 + gate_pre * (1.0 - sigmoid_gate))

    total = 0
    pulled_parts = []
    returned = []
    for group in groups:
        begin, end = group[0] * capacity, (group[-1] + 1) * capacity
        rows = jnp.concatenate([arrived[k] for k in group], axis=0)
        columns = [
            lax.dynamic_slice_in_dim(rows, (mine ^ j) * share, share, 1) for j in range(replicas)
        ]
        left = [columns[0]] + [swap(columns[j], "rep", j) for j in range(1, replicas)]
        right = [hidden_of[j][begin:end] for j in range(replicas)]
        total = total + lax.dot_general(
            jnp.concatenate(left, axis=0),
            jnp.concatenate(right, axis=0),
            (((0,), (0,)), ((), ())),
            preferred_element_type=jnp.float32,
        )
        pulled = jnp.dot(rows, down_weight[0], preferred_element_type=jnp.float32)
        pulled_parts.append(pulled)
        router = jnp.sum(pulled * hidden[begin:end], axis=1).reshape(len(group), capacity)
        returned += [router[i] if k == 0 else swap(router[i], "exp", k) for i, k in enumerate(group)]
    pulled = jnp.concatenate(pulled_parts, axis=0)
    pair_grads = jnp.concatenate([pulled * gate_factor, pulled * silu_gate], axis=1).astype(
        jnp.bfloat16
    )
    pair_grads = pair_grads.reshape(peers, capacity, 2 * width)
    pair_grads = jnp.take(pair_grads, jnp.arange(peers) ^ me, axis=0)
    returned_grad = jnp.concatenate(returned, axis=0)
    token_grad = jnp.sum(jnp.where(placement, returned_grad[:, None], 0.0), axis=0)
    token_grad = token_grad / weight.astype(jnp.float32)
    return (
        total[None],
        pair_grads.reshape(1, 1, rows_all, 2 * width),
        token_grad[:, None],
    )


def solution(mesh):
    in_specs = (
        P(("rep", "exp"), None),
        P(("rep", "exp"), None),
        P(("rep", "exp"), None),
        P("exp", None, None),
        P("rep", "exp", None, None),
    )
    out_specs = (P("exp", "rep", None), P("rep", "exp", None, None), P(("rep", "exp"), None))
    return jax.shard_map(shards, mesh=mesh, in_specs=in_specs, out_specs=out_specs, check_vma=False)
```

```python
import jax
import jax.numpy as jnp
from jax import lax
from jax.experimental import pallas as pl
from jax.experimental.pallas import tpu as pltpu
from jax.sharding import PartitionSpec as P

WHOLE_VMEM = pl.BlockSpec(memory_space=pltpu.VMEM)
IN_PLACE = pl.BlockSpec(memory_space=pl.ANY)
SMALL = pl.CostEstimate(flops=1024, bytes_accessed=1024, transcendentals=0)
LARGE = pl.CostEstimate(flops=10**10, bytes_accessed=1024, transcendentals=0)


def swap(value, axis, step):
    n = lax.axis_size(axis)
    return lax.ppermute(value, axis, [(i, i ^ step) for i in range(n)])


def kernel_call(kernel, outs, operands, name, cost=SMALL, vmem=24, **more):
    more.setdefault("in_specs", [WHOLE_VMEM] * len(operands))
    more.setdefault("out_specs", [WHOLE_VMEM] * len(outs))
    return pl.pallas_call(
        kernel,
        out_shape=outs,
        compiler_params=pltpu.CompilerParams(vmem_limit_bytes=vmem * 1024 * 1024),
        cost_estimate=cost,
        name=name,
        **more,
    )(*operands)


def copy_kernel(rows, out):
    out[...] = rows[...]


def hidden_kernel(saved, hidden):
    for k in range(saved.shape[0]):
        gate, up, sigmoid = gate_parts(saved[k])
        hidden[k] = (gate * sigmoid * up).astype(jnp.bfloat16)


def place_kernel(cap, order, cot, cot_sib, routes, routes_sib, weights, weights_sib, *outs):
    chips = len(order)
    blocks, slots_out, last_out = outs[:chips], outs[chips], outs[chips + 1]
    me, mine = lax.axis_index("exp"), lax.axis_index("rep")
    chip, core = me // 2, lax.rem(me, 2)
    replicas, pair, share = blocks[0].shape
    tokens = cot.shape[0]
    before = (
        lax.broadcasted_iota(jnp.int32, (tokens, tokens), 0)
        < lax.broadcasted_iota(jnp.int32, (tokens, tokens), 1)
    ).astype(jnp.bfloat16)
    placements = []
    for i, (ids, gains) in enumerate(((routes, weights), (routes_sib, weights_sib))):
        expert = ids[...]
        weight = gains[...].astype(jnp.bfloat16).astype(jnp.float32)
        hot = lax.broadcasted_iota(jnp.int32, (2 * chips, tokens), 0) == expert
        earlier = jnp.dot(hot.astype(jnp.bfloat16), before, preferred_element_type=jnp.float32)
        position = jnp.sum(jnp.where(hot, earlier, 0.0), axis=0, keepdims=True).astype(jnp.int32)
        source = core if i == 0 else 1 - core
        step = (expert >> 1) ^ chip
        same = (expert & 1) == core
        rank = sum(jnp.where(step == k, i, 0) for i, k in enumerate(order))
        slot = jnp.where(same, rank * pair + source * cap + position, -1)
        slots_out[i : i + 1, :] = slot
        if i == 0:
            last_out[...] = jnp.where(
                step == order[-1], jnp.where(same, position, cap + position), -1
            )
        here = lax.broadcasted_iota(jnp.int32, (chips * pair, tokens), 0) == slot
        placements.append(jnp.where(here, weight, 0.0).astype(jnp.bfloat16))
    placement = jnp.concatenate(placements, axis=1)
    for j in range(replicas):
        columns = pl.ds(pl.multiple_of((mine ^ j) * share, share), share)
        rows = jnp.concatenate([cot[:, columns], cot_sib[:, columns]], axis=0)
        sent = jnp.dot(placement, rows, preferred_element_type=jnp.float32).astype(jnp.bfloat16)
        for k in range(chips):
            blocks[k][j] = sent[k * pair : (k + 1) * pair]


def products(arrived, down):
    mine = lax.axis_index("rep")
    replicas, _, share = arrived[0].shape
    pulled = 0
    for j in range(replicas):
        rows = jnp.concatenate([ref[j] for ref in arrived], axis=0)
        begin = pl.multiple_of((mine ^ j) * share, share)
        pulled += jnp.dot(rows, down[0, pl.ds(begin, share), :], preferred_element_type=jnp.float32)
    return pulled


def gate_parts(saved):
    width = saved.shape[1] // 2
    gate, up = saved[:, :width].astype(jnp.float32), saved[:, width:].astype(jnp.float32)
    sigmoid = 1.0 / (1.0 + jnp.exp(-gate))
    return gate, up, sigmoid


def router_sums(pulled, saved):
    gate, up, sigmoid = gate_parts(saved)
    return lax.dot_general(
        jnp.ones((8, pulled.shape[1]), jnp.float32),
        pulled * (gate * sigmoid * up),
        (((1,), (1,)), ((), ())),
        precision=lax.Precision.HIGHEST,
        preferred_element_type=jnp.float32,
    )[0:1]


def pair_grads(pulled, saved):
    gate, up, sigmoid = gate_parts(saved)
    both = [pulled * up * sigmoid * (1.0 + gate * (1.0 - sigmoid)), pulled * (gate * sigmoid)]
    return jnp.concatenate(both, axis=1).astype(jnp.bfloat16)


def pull_early_kernel(steps, *refs):
    count = len(steps)
    arrived, (down, saved, grads), routers = refs[:count], refs[count : count + 3], refs[count + 3 :]
    chip = lax.axis_index("exp") // 2
    pulled = products(arrived, down)
    pair = arrived[0].shape[1]
    for i, k in enumerate(steps):
        part = pulled[i * pair : (i + 1) * pair]
        routers[i][...] = router_sums(part, saved[chip ^ k])
        grads[chip ^ k] = pair_grads(part, saved[chip ^ k])


def pull_last_kernel(step, arrived, down, saved, pulled, same, other):
    me = lax.axis_index("exp")
    chip, core = me // 2, lax.rem(me, 2)
    pulled[...] = products([arrived], down)
    router = router_sums(pulled[...], saved[chip ^ step])
    cap = router.shape[1] // 2
    same[...] = jnp.where(core == 0, router[:, :cap], router[:, cap:])
    other[...] = jnp.where(core == 0, router[:, cap:], router[:, :cap])


def stack_kernel(count, *refs):
    for j, out in enumerate(refs[count:]):
        out[...] = jnp.concatenate([ref[j] for ref in refs[:count]], axis=0)


def stack(rows):
    replicas, pair, share = rows[0].shape
    return kernel_call(
        lambda *refs: stack_kernel(len(rows), *refs),
        [jax.ShapeDtypeStruct((len(rows) * pair, share), jnp.bfloat16)] * replicas,
        rows,
        "stack",
    )


def units_kernel(order, *refs):
    hidden, early, late = refs[-3::-1], refs[-2], refs[-1]
    chip = lax.axis_index("exp") // 2
    early[...] = jnp.concatenate([ref[chip ^ k] for ref in hidden for k in order[:-1]], axis=0)
    late[...] = jnp.concatenate([ref[chip ^ order[-1]] for ref in hidden], axis=0)


def weight_early_kernel(first, rows, units, before, out):
    size = rows[0].shape[0]
    total = lax.dot_general(
        jnp.concatenate([ref[...] for ref in rows], axis=0),
        units[first * size : (first + len(rows)) * size, :],
        (((0,), (0,)), ((), ())),
        preferred_element_type=jnp.float32,
    )
    out[...] = total + before[0][...] if before else total


def finish_kernel(step, replicas, parts, *refs):
    rows = refs[:replicas]
    units, early, pulled, saved, _, out, grads, held, held_grads, sems = refs[replicas:]
    size = early.shape[0] // parts
    copies = []
    for i in range(parts):
        span = pl.ds(i * size, size)
        left = jnp.concatenate([ref[:, i * size : (i + 1) * size] for ref in rows], axis=0)
        held[span, :] = early[span, :] + lax.dot_general(
            left, units[...], (((0,), (0,)), ((), ())), preferred_element_type=jnp.float32
        )
        copies.append(pltpu.make_async_copy(held.at[span, :], out.at[0, span, :], sems.at[i]))
        copies[-1].start()
        if i == 0:
            place = (lax.axis_index("exp") // 2) ^ step
            held_grads[...] = pair_grads(pulled[...], saved[place])
            copies.append(pltpu.make_async_copy(held_grads, grads.at[place], sems.at[parts]))
            copies[-1].start()
    for copy in copies:
        copy.wait()


def token_kernel(same, other, last_slots, own, sib, weights, out):
    values = jnp.concatenate([same[...], other[...]], axis=1)
    hot = lax.broadcasted_iota(jnp.int32, (values.shape[1], out.shape[1]), 0) == last_slots[...]
    found = lax.dot_general(
        jnp.broadcast_to(values, (8, values.shape[1])),
        hot.astype(jnp.float32),
        (((1,), (0,)), ((), ())),
        precision=lax.Precision.HIGHEST,
        preferred_element_type=jnp.float32,
    )[0:1]
    weight = weights[...].astype(jnp.bfloat16).astype(jnp.float32)
    out[...] = (own[...] + sib[...] + found) / weight


def shards(cotangent, routes, gate_weight, down_weight, saved_pre):
    peers = lax.axis_size("exp")
    replicas = lax.axis_size("rep")
    rows_all = saved_pre.shape[2]
    cap = rows_all // peers
    chips = peers // 2
    pair = 2 * cap
    if pair % 16:
        return plain_shards(cotangent, routes, gate_weight, down_weight, saved_pre)
    width = down_weight.shape[2]
    tokens, model = cotangent.shape
    share = model // replicas

    last = chips // 2
    early = [k for k in range(chips) if k != last]
    order = early + [last]

    routes = routes.reshape(1, tokens)
    weights = gate_weight.reshape(1, tokens)
    cot_sib = swap(cotangent, "exp", 1)
    routes_sib = swap(routes, "exp", 1)
    weights_sib = swap(weights, "exp", 1)
    own_rows = kernel_call(
        copy_kernel,
        [jax.ShapeDtypeStruct((tokens, model), jnp.bfloat16)],
        [cotangent],
        "own_rows",
        LARGE,
    )[0]
    *blocks, slots, last_slots = kernel_call(
        lambda *refs: place_kernel(cap, order, *refs),
        [jax.ShapeDtypeStruct((replicas, pair, share), jnp.bfloat16)] * chips
        + [
            jax.ShapeDtypeStruct((2, tokens), jnp.int32),
            jax.ShapeDtypeStruct((1, tokens), jnp.int32),
        ],
        [own_rows, cot_sib, routes, routes_sib, weights, weights_sib],
        "place",
    )

    blocks = dict(zip(order, blocks))
    arrived = {0: blocks[0]}
    for k in reversed(early[1:]):
        arrived[k] = swap(blocks[k], "exp", 2 * k)
    saved = saved_pre.reshape(chips, pair, 2 * width)
    saved, slots = lax.optimization_barrier((saved, slots))
    hidden = kernel_call(
        hidden_kernel,
        [jax.ShapeDtypeStruct((chips, pair, width), jnp.bfloat16)],
        [saved],
        "hidden",
    )[0]
    hidden_of = [hidden] + [swap(hidden, "rep", j) for j in range(1, replicas)]
    units, units_last = kernel_call(
        lambda *refs: units_kernel(order, *refs),
        [
            jax.ShapeDtypeStruct((replicas * len(early) * pair, width), jnp.bfloat16),
            jax.ShapeDtypeStruct((replicas * pair, width), jnp.bfloat16),
        ],
        hidden_of[::-1],
        "units",
    )

    rows, last_block, units = lax.optimization_barrier(
        ([arrived[k] for k in early], blocks[last], units)
    )
    arrived = dict(zip(early, rows))
    last_rows = swap(last_block, "exp", 2 * last)
    early_rows = stack(rows)
    early_rows = [early_rows[0]] + [swap(early_rows[j], "rep", j) for j in range(1, replicas)]
    grads, *routers = kernel_call(
        lambda *refs: pull_early_kernel(early, *refs),
        [jax.ShapeDtypeStruct(saved.shape, jnp.bfloat16)]
        + [jax.ShapeDtypeStruct((1, pair), jnp.float32)] * len(early),
        [*[arrived[k] for k in early], down_weight, saved],
        "pull_early",
    )
    returned = routers[:1] + [swap(router, "exp", 2 * k) for router, k in zip(routers[1:], early[1:])]
    total = []
    half = replicas // 2
    for first, count in ((0, half), (half, replicas - half)):
        total = kernel_call(
            lambda *refs: weight_early_kernel(
                first, refs[:count], refs[count], refs[count + 1 : -1], refs[-1]
            ),
            [jax.ShapeDtypeStruct((share, width), jnp.float32)],
            [*early_rows[first : first + count], units, *total],
            "weight_rest" if first else "weight_first",
        )
    total = total[0]

    rows, grads, total, near_returned = lax.optimization_barrier(
        (last_rows, grads, total, returned[:2])
    )
    returned = [*near_returned, *returned[2:]]
    late_rows = [rows[0]] + [swap(rows[j], "rep", j) for j in range(1, replicas)]
    returned = jnp.concatenate(returned, axis=1).reshape(len(early) * pair, 1)
    slot_index = lax.broadcasted_iota(jnp.int32, (len(early) * pair, 1), 0)
    sums = [
        jnp.sum(jnp.where(slot_index == ids, returned, 0.0), axis=0, keepdims=True)
        for ids in (slots[0:1], slots[1:2])
    ]
    rows, sums = lax.optimization_barrier((rows, sums))
    pulled, *routers = kernel_call(
        lambda *refs: pull_last_kernel(last, *refs),
        [jax.ShapeDtypeStruct((pair, width), jnp.float32)]
        + [jax.ShapeDtypeStruct((1, cap), jnp.float32)] * 2,
        [rows, down_weight, saved],
        "pull_last",
    )
    returned_last = [swap(routers[i], "exp", 2 * last + i) for i in range(2)]
    late_rows, sum_sib = lax.optimization_barrier((late_rows, sums[1]))
    sum_sib = swap(sum_sib, "exp", 1)
    parts = 4
    weight_grad, grads = kernel_call(
        lambda *refs: finish_kernel(last, replicas, parts, *refs),
        [
            jax.ShapeDtypeStruct((1, share, width), jnp.float32),
            jax.ShapeDtypeStruct(saved.shape, jnp.bfloat16),
        ],
        [*late_rows, units_last, total, pulled, saved, grads],
        "finish",
        LARGE,
        in_specs=[WHOLE_VMEM] * (replicas + 4) + [IN_PLACE],
        out_specs=[IN_PLACE] * 2,
        input_output_aliases={replicas + 4: 1},
        scratch_shapes=[
            pltpu.VMEM((share, width), jnp.float32),
            pltpu.VMEM((pair, 2 * width), jnp.bfloat16),
            pltpu.SemaphoreType.DMA((parts + 1,)),
        ],
    )
    returned_last, weight_grad = lax.optimization_barrier((returned_last, weight_grad))
    token_grad = kernel_call(
        token_kernel,
        [jax.ShapeDtypeStruct((1, tokens), jnp.float32)],
        [*returned_last, last_slots, sums[0], sum_sib, weights],
        "token",
    )[0]
    return (weight_grad, grads.reshape(1, 1, rows_all, 2 * width), token_grad.reshape(tokens, 1))


def plain_shards(cotangent, routes, gate_weight, down_weight, saved_pre):
    peers = lax.axis_size("exp")
    replicas = lax.axis_size("rep")
    me = lax.axis_index("exp")
    mine = lax.axis_index("rep")
    rows_all = saved_pre.shape[2]
    capacity = rows_all // peers
    width = down_weight.shape[2]
    model = cotangent.shape[1]
    share = model // replicas

    expert_ids = routes[:, 0]
    experts = lax.broadcasted_iota(jnp.int32, (1, peers), 1)
    one_hot = (expert_ids[:, None] == experts).astype(jnp.int32)
    earlier = jnp.cumsum(one_hot, axis=0) - one_hot
    position = jnp.sum(earlier * one_hot, axis=1)
    slot_ids = (expert_ids ^ me) * capacity + position
    slot_index = lax.broadcasted_iota(jnp.int32, (rows_all, 1), 0)
    placement = slot_index == slot_ids[None, :]
    weight = gate_weight[:, 0].astype(jnp.bfloat16)
    outgoing = jnp.dot(
        jnp.where(placement, weight[None, :], 0), cotangent, preferred_element_type=jnp.float32
    ).astype(jnp.bfloat16)
    outgoing = outgoing.reshape(peers, capacity, model)

    groups = [
        list(range(0, peers // 2)),
        list(range(peers // 2, peers // 4 * 3)),
        list(range(peers // 4 * 3, peers)),
    ]
    arrived = {0: outgoing[0]}
    for k in groups[1] + groups[2] + groups[0][1:]:
        arrived[k] = swap(outgoing[k], "exp", k)

    saved = saved_pre[0, 0].reshape(peers, capacity, 2 * width)
    saved = jnp.take(saved, jnp.arange(peers) ^ me, axis=0).reshape(rows_all, 2 * width)
    saved = saved.astype(jnp.float32)
    gate_pre = saved[:, :width]
    up_pre = saved[:, width:]
    sigmoid_gate = jax.nn.sigmoid(gate_pre)
    silu_gate = gate_pre * sigmoid_gate
    hidden = silu_gate * up_pre
    hidden_sent = hidden.astype(jnp.bfloat16)
    hidden_of = [hidden_sent] + [swap(hidden_sent, "rep", j) for j in range(1, replicas)]
    gate_factor = up_pre * sigmoid_gate * (1.0 + gate_pre * (1.0 - sigmoid_gate))

    total = 0
    pulled_parts = []
    returned = []
    for group in groups:
        begin, end = group[0] * capacity, (group[-1] + 1) * capacity
        rows = jnp.concatenate([arrived[k] for k in group], axis=0)
        columns = [
            lax.dynamic_slice_in_dim(rows, (mine ^ j) * share, share, 1) for j in range(replicas)
        ]
        left = [columns[0]] + [swap(columns[j], "rep", j) for j in range(1, replicas)]
        right = [hidden_of[j][begin:end] for j in range(replicas)]
        total = total + lax.dot_general(
            jnp.concatenate(left, axis=0),
            jnp.concatenate(right, axis=0),
            (((0,), (0,)), ((), ())),
            preferred_element_type=jnp.float32,
        )
        pulled = jnp.dot(rows, down_weight[0], preferred_element_type=jnp.float32)
        pulled_parts.append(pulled)
        router = jnp.sum(pulled * hidden[begin:end], axis=1).reshape(len(group), capacity)
        returned += [router[i] if k == 0 else swap(router[i], "exp", k) for i, k in enumerate(group)]
    pulled = jnp.concatenate(pulled_parts, axis=0)
    pair_grads = jnp.concatenate([pulled * gate_factor, pulled * silu_gate], axis=1).astype(
        jnp.bfloat16
    )
    pair_grads = pair_grads.reshape(peers, capacity, 2 * width)
    pair_grads = jnp.take(pair_grads, jnp.arange(peers) ^ me, axis=0)
    returned_grad = jnp.concatenate(returned, axis=0)
    token_grad = jnp.sum(jnp.where(placement, returned_grad[:, None], 0.0), axis=0)
    token_grad = token_grad / weight.astype(jnp.float32)
    return (
        total[None],
        pair_grads.reshape(1, 1, rows_all, 2 * width),
        token_grad[:, None],
    )


def solution(mesh):
    in_specs = (
        P(("rep", "exp"), None),
        P(("rep", "exp"), None),
        P(("rep", "exp"), None),
        P("exp", None, None),
        P("rep", "exp", None, None),
    )
    out_specs = (P("exp", "rep", None), P("rep", "exp", None, None), P(("rep", "exp"), None))
    return jax.shard_map(shards, mesh=mesh, in_specs=in_specs, out_specs=out_specs, check_vma=False)
```
